128 devices in a mesh: seq: 128 (over x, z, y, core).
Axes of the slice: x: 4, y: 4, z: 4, core: 2. Of those that a mesh axis runs over, the one named last changes fastest.
Arguments:
- queries: bfloat16 [16384, 1280], P('seq'), may hold values from -6 to 6
- key_states: bfloat16 [16384, 1280], P('seq'), may hold values from -6 to 6
- value_states: bfloat16 [16384, 1280], P('seq'), may hold values from -6 to 6
- offsets: int32 [2, 16], replicated, may hold values from 0 to 31, as said below
- out_weight: bfloat16 [1280, 1280], replicated, may hold values from -0.15625 to 0.15625
Outputs:
- attended: bfloat16 [16384, 1280], P('seq')
The draws below stay inside these ranges and needn't reach their ends.
Inputs may be any that keep to these rules, and one draw needn't show every extreme that they name: `offsets`: offsets in row 0 are below 8, those in row 1 below 32.
All inputs are finite; a program needn't handle non-finite values.
Results may differ from the reference program's by a relative error of at most 0.0054.
Values may be sent and summed in bfloat16 or wider, within the bound.
No kernel may reach another device: no remote copies, remote signals or barrier semaphores. Data moves between devices by JAX's collectives and lax.ppermute only.
A program may use at most 128 MiB of HBM per device.

```python
import jax
import jax.numpy as jnp
from jax import lax

HEAD_COUNT = 16
HDIM = 80
D = 1280
SEG1 = 2048
SECOND_DILATION = 8
THIRD_DILATION = 32
TOKEN_COUNT = 16384
MIDDLE_SEGMENT = 16384


def draw_queries(key, part):
    key = jax.random.fold_in(key, 7)
    return jnp.clip(jax.random.normal(key, (TOKEN_COUNT, D), jnp.float32), -4.0, 4.0).astype(jnp.bfloat16)


def draw_key_states(key, part):
    key = jax.random.fold_in(key, 11)
    return jnp.clip(jax.random.normal(key, (TOKEN_COUNT, D), jnp.float32), -4.0, 4.0).astype(jnp.bfloat16)


def draw_offsets(key, part):
    key = jax.random.fold_in(key, 5)
    divide_random_keys = jax.random.split(key, 4)
    middle_level = jax.random.randint(divide_random_keys[0], (HEAD_COUNT,), 0, SECOND_DILATION)
    distant_level = jax.random.randint(divide_random_keys[1], (HEAD_COUNT,), 0, THIRD_DILATION)
    low_head = jax.random.randint(divide_random_keys[2], (), 0, HEAD_COUNT)
    upper_head = jax.random.randint(divide_random_keys[3], (), 0, HEAD_COUNT)
    head_numbers = jnp.arange(HEAD_COUNT)
    middle_level = jnp.where(head_numbers == low_head, 0, middle_level)
    distant_level = jnp.where(head_numbers == upper_head, THIRD_DILATION - 1, distant_level)
    return jnp.stack([middle_level, distant_level]).astype(jnp.int32)


def levels(own_key, extent, shards, low, top_value):
    def one(dim, blocks):
        draws = jax.random.uniform(jax.random.fold_in(jax.random.fold_in(own_key, 6), dim), (blocks,), jnp.float32, low / len(shards), top_value / len(shards))
        return jnp.repeat(jnp.exp(draws), extent[dim] // blocks).reshape((-1,) + (1,) * (len(extent) - dim - 1))

    gain = one(*shards[0])
    for cut in shards[1:]:
        gain = gain * one(*cut)
    return gain


def bell_draw(own_key, dims, width, limit, cuts=(), kind=jnp.bfloat16):
    entries = width * jax.random.normal(own_key, dims, jnp.float32)
    if cuts:
        entries = entries * levels(own_key, dims, cuts, -0.22, 0.18)
    return jnp.clip(entries, -limit, limit).astype(kind)


def setup_inputs(seed: int = 0) -> dict:
    seeds = jax.random.split(jax.random.key(seed), 6)
    queries = draw_queries(jax.random.fold_in(seeds[5], 71), 0)
    key_states = draw_key_states(jax.random.fold_in(seeds[5], 71), 0)
    value_states = bell_draw(seeds[2], (TOKEN_COUNT, D), 1.0, 6.0, ((0, 128),))
    offsets = draw_offsets(jax.random.fold_in(seeds[5], 71), 0)
    out_weight = bell_draw(seeds[4], (D, D), D ** -0.5, 0.15625)
    return dict(queries=queries, key_states=key_states, value_states=value_states, offsets=offsets, out_weight=out_weight)


def select_dilated(source, chosen_off, stride):
    grouped = source.reshape(source.shape[0] // stride, stride, HEAD_COUNT, HDIM)
    chosen = jnp.arange(stride)[None, :, None, None] == chosen_off[None, None, :, None]
    return jnp.sum(jnp.where(chosen, grouped, jnp.zeros((), source.dtype)), axis=1), chosen


def spread(level_out, log_total, chosen):
    full_out = jnp.where(chosen, level_out[:, None], jnp.zeros((), jnp.float32)).reshape(-1, HEAD_COUNT, HDIM)
    full_log = jnp.where(chosen[..., 0], log_total[:, None, :], -jnp.inf).reshape(-1, HEAD_COUNT)
    return full_out, full_log


def segment_attention(query_sel, key_sel, value_sel, seg_rows):
    n_blocks = query_sel.shape[0] // seg_rows

    def per_block(block_in):
        query_b, key_b, value_b = block_in
        scores = jnp.einsum('qhd,khd->hqk', query_b.astype(jnp.float32), key_b.astype(jnp.float32)) * (HDIM ** -0.5)
        causal = jnp.arange(seg_rows)[:, None] >= jnp.arange(seg_rows)[None, :]
        scores = jnp.where(causal[None], scores, -jnp.inf)
        highest = jnp.max(scores, axis=-1, keepdims=True)
        expd = jnp.exp(scores - highest)
        totals = jnp.sum(expd, axis=-1)
        weights = expd.astype(jnp.bfloat16)
        output = jnp.einsum('hqk,khd->qhd', weights.astype(jnp.float32), value_b.astype(jnp.float32)) / totals.T[:, :, None]
        log_total = (highest[..., 0] + jnp.log(totals)).T
        return output, log_total

    blocks = tuple(a.reshape(n_blocks, seg_rows, HEAD_COUNT, HDIM) for a in (query_sel, key_sel, value_sel))
    output, log_total = lax.map(per_block, blocks)
    return output.reshape(-1, HEAD_COUNT, HDIM), log_total.reshape(-1, HEAD_COUNT)


def combine(outputs, logs):
    peak = jnp.maximum(jnp.maximum(logs[0], logs[1]), logs[2])
    shares = [jnp.exp(one_log - peak) for one_log in logs]
    numer = shares[0][..., None] * outputs[0] + shares[1][..., None] * outputs[1] + shares[2][..., None] * outputs[2]
    return numer / (shares[0] + shares[1] + shares[2])[..., None]


def reference(queries, key_states, value_states, offsets, out_weight):
    query_per_head = queries.reshape(TOKEN_COUNT, HEAD_COUNT, HDIM)
    key_per_head = key_states.reshape(TOKEN_COUNT, HEAD_COUNT, HDIM)
    value_per_head = value_states.reshape(TOKEN_COUNT, HEAD_COUNT, HDIM)
    out_near, log_near = segment_attention(query_per_head, key_per_head, value_per_head, SEG1)
    middle_query, selected_middle = select_dilated(query_per_head, offsets[0], SECOND_DILATION)
    middle_key, unused_result = select_dilated(key_per_head, offsets[0], SECOND_DILATION)
    middle_value, unused_result = select_dilated(value_per_head, offsets[0], SECOND_DILATION)
    middle_output, middle_logsum = segment_attention(middle_query, middle_key, middle_value, MIDDLE_SEGMENT // SECOND_DILATION)
    middle_output, middle_logsum = spread(middle_output, middle_logsum, selected_middle)
    distant_query, selected_distant = select_dilated(query_per_head, offsets[1], THIRD_DILATION)
    distant_key, unused_result = select_dilated(key_per_head, offsets[1], THIRD_DILATION)
    distant_value, unused_result = select_dilated(value_per_head, offsets[1], THIRD_DILATION)
    distant_output, distant_logsum = segment_attention(distant_query, distant_key, distant_value, TOKEN_COUNT // THIRD_DILATION)
    distant_output, distant_logsum = spread(distant_output, distant_logsum, selected_distant)
    mixture = combine((out_near, middle_output, distant_output), (log_near, middle_logsum, distant_logsum))
    mixture = mixture.reshape(TOKEN_COUNT, D).astype(jnp.bfloat16)
    return jnp.dot(mixture, out_weight, preferred_element_type=jnp.float32).astype(jnp.bfloat16)
```

```python
import functools
import math

import jax
import jax.numpy as jnp
from jax import lax
from jax.experimental import pallas as pl
from jax.experimental.pallas import tpu as pltpu
from jax.sharding import PartitionSpec as P

HEADS = 16
HDIM = 80
SEG1 = 2048
SEGS = 8
ROWS = 128
D2 = 8
D3 = 32
C2 = SEG1 // D2
C3 = SEG1 // D3
ROW_L = HDIM
ROW_M = HDIM + 8
AUG = HDIM + 16
SCALE = math.log2(math.e) / math.sqrt(HDIM)
LOW = -1e30
BF = jnp.bfloat16
F32 = jnp.float32


def contract0(a, b):
    return lax.dot_general(a, b, (((0,), (0,)), ((), ())), preferred_element_type=F32)


def dot(a, b):
    return jnp.dot(a, b, preferred_element_type=F32)


def iota(shape, dim):
    return lax.broadcasted_iota(jnp.int32, shape, dim)


def onehot(cond):
    return jnp.where(cond, 1.0, 0.0).astype(BF)


def my_offsets(off_ref):
    head = lax.rem(lax.axis_index("seq"), HEADS)
    return off_ref[0, head], off_ref[1, head]


def blocks(ref, first, low, high):
    return jnp.concatenate([ref[s, low:high, :] for s in range(first, first + 8)], axis=1)


def pack_kernel(q_ref, k_ref, v_ref, out_ref):
    for part, ref in enumerate((q_ref, k_ref, v_ref)):
        for col in range(0, HEADS * HDIM, 640):
            turned = ref[:, col : col + 640].T
            for n in range(8):
                out_ref[col // HDIM + n, part * HDIM : (part + 1) * HDIM, :] = turned[
                    n * HDIM : (n + 1) * HDIM
                ]


def select_kernel(off_ref, x_ref, kv_ref):
    off2, off3 = my_offsets(off_ref)
    tok = iota((1024, 128), 0)
    lane = iota((1024, 128), 1)
    pick2 = onehot(tok == lane * D2 + off2)
    far = jnp.zeros((HDIM, 128), F32)
    for half in range(2):
        kv = blocks(x_ref, 8 * half, HDIM, 3 * HDIM)
        got = dot(kv, pick2).astype(BF)
        kv_ref[half * HDIM : (half + 1) * HDIM, :] = got[:HDIM]
        kv_ref[(2 + half) * HDIM : (3 + half) * HDIM, :] = got[HDIM:]
        tok3 = tok + half * 1024 - off3
        far = far + dot(kv[:HDIM], onehot(tok3 == lane * D3))
        far = far + dot(kv[HDIM:], onehot(tok3 == (lane - 64) * D3))
    kv_ref[4 * HDIM :, :] = far.astype(BF)


def near_kernel(off_ref, x_ref, state_ref, q_ref):
    ones = jnp.ones((16, 256), BF)
    for qi in range(8):
        q_t = jnp.concatenate([x_ref[2 * qi + s, :HDIM, :] for s in range(2)], axis=1)
        parts = []
        for ki in range(qi + 1):
            k_t = jnp.concatenate(
                [x_ref[2 * ki + s, HDIM : 2 * HDIM, :] for s in range(2)], axis=1
            )
            scores = contract0(k_t, q_t)
            if ki == qi:
                scores = jnp.where(iota((256, 256), 0) <= iota((256, 256), 1), scores, LOW)
            parts.append(scores)
        high = functools.reduce(
            jnp.maximum, [jnp.max(p, axis=0, keepdims=True) for p in parts]
        ) * SCALE
        acc = jnp.zeros((AUG, 256), F32)
        for ki in range(qi + 1):
            v_t = jnp.concatenate(
                [x_ref[2 * ki + s, 2 * HDIM : 3 * HDIM, :] for s in range(2)], axis=1
            )
            weights = jnp.exp2(parts[ki] * SCALE - high).astype(BF)
            acc = acc + dot(jnp.concatenate([v_t, ones], axis=0), weights)
        cols = slice(qi * 256, (qi + 1) * 256)
        state_ref[:ROW_M, cols] = acc[:ROW_M]
        state_ref[ROW_M:, cols] = jnp.broadcast_to(high, (8, 256))
    off2, off3 = my_offsets(off_ref)
    tok = iota((1024, 128), 0)
    lane = iota((1024, 128), 1)
    pick2 = onehot(tok == lane * D2 + off2)
    far = jnp.zeros((HDIM, 128), F32)
    for half in range(2):
        q_t = blocks(x_ref, 8 * half, 0, HDIM)
        q_ref[half * HDIM : (half + 1) * HDIM, :] = dot(q_t, pick2).astype(BF)
        far = far + dot(q_t, onehot(tok + half * 1024 == lane * D3 + off3))
    q_ref[2 * HDIM :, :] = far.astype(BF)


def split3(x):
    top = x.astype(BF)
    rest = x - top.astype(F32)
    mid = rest.astype(BF)
    return top, mid, (rest - mid.astype(F32)).astype(BF)


def spread(acc, high, place):
    top, mid, _ = split3(acc[:HDIM])
    stat = jnp.concatenate(
        [acc[ROW_L : ROW_L + 8], jnp.broadcast_to(high, (8, high.shape[1]))], axis=0
    )
    stats = split3(stat)
    out = dot(jnp.concatenate((top, mid) + stats, axis=0), place)
    base = 2 * HDIM
    stat = out[base : base + 16] + out[base + 16 : base + 32] + out[base + 32 : base + 48]
    return out[:HDIM] + out[HDIM : 2 * HDIM], stat[:1], stat[8:9]


def far_kernel(off_ref, state_ref, q_ref, *refs):
    pieces, out_ref = refs[:-1], refs[-1]
    off2, off3 = my_offsets(off_ref)
    seg = lax.axis_index("seq") // HEADS
    q2 = jnp.concatenate([q_ref[:HDIM, :], q_ref[HDIM : 2 * HDIM, :]], axis=1)
    row = iota((C2, C2), 0)
    col = iota((C2, C2), 1)
    parts = []
    for back, piece in enumerate(pieces):
        k_t = jnp.concatenate([piece[:HDIM, :], piece[HDIM : 2 * HDIM, :]], axis=1)
        scores = contract0(k_t, q2)
        if back == 0:
            scores = jnp.where(row <= col, scores, LOW)
        else:
            scores = jnp.where(seg >= back, scores, LOW)
        parts.append(scores)
    high2 = functools.reduce(
        jnp.maximum, [jnp.max(p, axis=0, keepdims=True) for p in parts]
    ) * SCALE
    acc2 = jnp.zeros((AUG, C2), F32)
    ones = jnp.ones((16, C2), BF)
    for piece, scores in zip(pieces, parts):
        v_t = jnp.concatenate(
            [piece[2 * HDIM : 3 * HDIM, :], piece[3 * HDIM : 4 * HDIM, :]], axis=1
        )
        weights = jnp.exp2(scores * SCALE - high2).astype(BF)
        acc2 = acc2 + dot(jnp.concatenate([v_t, ones], axis=0), weights)
    q3 = q_ref[2 * HDIM :, :]
    row = iota((C3, 128), 0)
    col = iota((C3, 128), 1)
    parts = []
    for back, piece in enumerate(pieces):
        scores = contract0(piece[4 * HDIM :, :], q3)[:C3]
        if back == 0:
            scores = jnp.where(row <= col, scores, LOW)
        else:
            scores = jnp.where(seg >= back, scores, LOW)
        parts.append(scores)
    high3 = functools.reduce(
        jnp.maximum, [jnp.max(p, axis=0, keepdims=True) for p in parts]
    ) * SCALE
    acc3 = jnp.zeros((AUG, 128), F32)
    ones = jnp.ones((16, 128), BF)
    for piece, scores in zip(pieces, parts):
        weights = jnp.exp2(scores * SCALE - high3).astype(BF)
        weights = jnp.concatenate([jnp.zeros((C3, 128), BF), weights], axis=0)
        acc3 = acc3 + dot(jnp.concatenate([piece[4 * HDIM :, :], ones], axis=0), weights)
    lane = iota((128, 1024), 0)
    tok = iota((128, 1024), 1)
    place2 = onehot(tok == lane * D2 + off2)
    tok1 = iota((1, 1024), 1)
    for half in range(2):
        cols = slice(half * 1024, (half + 1) * 1024)
        near = state_ref[:, cols]
        part = slice(half * 128, (half + 1) * 128)
        sum2, tot2, hi2 = spread(acc2[:, part], high2[:, part], place2)
        place3 = onehot(tok + half * 1024 == lane * D3 + off3)
        sum3, tot3, hi3 = spread(acc3, high3, place3)
        hi1 = near[ROW_M : ROW_M + 1]
        hi2 = jnp.where(lax.rem(tok1, D2) == off2, hi2, LOW)
        hi3 = jnp.where(lax.rem(tok1, D3) == off3, hi3, LOW)
        peak = jnp.maximum(jnp.maximum(hi1, hi2), hi3)
        e1, e2, e3 = jnp.exp2(hi1 - peak), jnp.exp2(hi2 - peak), jnp.exp2(hi3 - peak)
        inv = 1.0 / (e1 * near[ROW_L : ROW_L + 1] + e2 * tot2 + e3 * tot3)
        mixed = near[:HDIM] * (e1 * inv) + sum2 * (e2 * inv) + sum3 * (e3 * inv)
        mixed = mixed.astype(BF)
        for s in range(8):
            out_ref[half * 8 + s] = mixed[:, s * 128 : (s + 1) * 128]


def call(kernel, out_shapes, smem, vmem):
    return pl.pallas_call(
        kernel,
        out_shape=out_shapes,
        in_specs=[pl.BlockSpec(memory_space=pltpu.SMEM)] * smem
        + [pl.BlockSpec(memory_space=pltpu.VMEM)] * vmem,
        out_specs=jax.tree.map(lambda _: pl.BlockSpec(memory_space=pltpu.VMEM), out_shapes),
        compiler_params=pltpu.CompilerParams(vmem_limit_bytes=40 * 2**20),
    )


def shape(*dims, dtype=BF):
    return jax.ShapeDtypeStruct(dims, dtype)


def on_device(queries, key_states, value_states, offsets, out_weight):
    near_groups = [[g * HEADS + i for i in range(HEADS)] for g in range(SEGS)]
    packed = call(pack_kernel, shape(HEADS, 3 * HDIM, ROWS), 0, 3)(
        queries, key_states, value_states
    )
    mine = lax.all_to_all(packed, "seq", 0, 0, axis_index_groups=near_groups, tiled=True)
    chosen = call(select_kernel, shape(5 * HDIM, 128), 1, 1)(offsets, mine)
    pieces = [chosen]
    for back in range(1, SEGS):
        pairs = [(i, (i + HEADS * back) % 128) for i in range(128)]
        pieces.append(lax.ppermute(chosen, "seq", pairs))
    state, chosen_q = call(
        near_kernel, (shape(AUG, SEG1, dtype=F32), shape(3 * HDIM, 128)), 1, 1
    )(offsets, mine)
    mixed = call(far_kernel, shape(HEADS, HDIM, ROWS), 1, 2 + SEGS)(
        offsets, state, chosen_q, *pieces
    )
    home = lax.all_to_all(mixed, "seq", 0, 0, axis_index_groups=near_groups, tiled=True)
    return contract0(home.reshape(HEADS * HDIM, ROWS), out_weight).astype(BF)


def solution(mesh):
    placed = (P("seq", None), P("seq", None), P("seq", None), P(), P())
    return jax.shard_map(
        on_device, mesh=mesh, in_specs=placed, out_specs=P("seq", None), check_vma=False
    )
```

```python
import functools
import math

import jax
import jax.numpy as jnp
from jax import lax
from jax.experimental import pallas as pl
from jax.experimental.pallas import tpu as pltpu
from jax.sharding import PartitionSpec as P

HEADS = 16
HDIM = 80
SEG1 = 2048
SEGS = 8
ROWS = 128
D2 = 8
D3 = 32
C2 = SEG1 // D2
C3 = SEG1 // D3
ROW_L = HDIM
ROW_M = HDIM + 8
AUG = HDIM + 16
SCALE = math.log2(math.e) / math.sqrt(HDIM)
LOW = -1e30
BF = jnp.bfloat16
F32 = jnp.float32


def contract0(a, b):
    return lax.dot_general(a, b, (((0,), (0,)), ((), ())), preferred_element_type=F32)


def dot(a, b):
    return jnp.dot(a, b, preferred_element_type=F32)


def iota(shape, dim):
    return lax.broadcasted_iota(jnp.int32, shape, dim)


def onehot(cond):
    return jnp.where(cond, 1.0, 0.0).astype(BF)


def my_offsets(off_ref):
    head = lax.rem(lax.axis_index("seq") // 2, HEADS)
    return off_ref[0, head], off_ref[1, head]


def blocks(ref, first, low, high):
    return jnp.concatenate([ref[s, low:high, :] for s in range(first, first + 8)], axis=1)


def pack_kernel(q_hbm, k_hbm, v_hbm, out_ref, held, sems):
    half = HEADS * HDIM // 2
    copies = []
    for part, ref in enumerate((q_hbm, k_hbm, v_hbm)):
        for n in range(2):
            cols = pl.ds(n * half, half)
            copy = pltpu.make_async_copy(
                ref.at[:, cols], held.at[part, :, cols], sems.at[2 * part + n]
            )
            copy.start()
            copies.append(copy)
    for part in range(3):
        for n in range(2):
            copies[2 * part + n].wait()
            turned = held[part, :, n * half : (n + 1) * half].T
            for m in range(8):
                out_ref[8 * n + m, part * HDIM : (part + 1) * HDIM, :] = turned[
                    m * HDIM : (m + 1) * HDIM
                ]


def select_kernel(off_ref, x_ref, kv_ref, all_ref):
    off2, off3 = my_offsets(off_ref)
    tok = iota((1024, 128), 0)
    lane = iota((1024, 128), 1)
    pick2 = onehot(tok == lane * D2 + off2)
    far = jnp.zeros((HDIM, 128), F32)
    for half in range(2):
        kv = blocks(x_ref, 8 * half, HDIM, 3 * HDIM)
        got = dot(kv, pick2).astype(BF)
        kv_ref[half * HDIM : (half + 1) * HDIM, :] = got[:HDIM]
        kv_ref[(2 + half) * HDIM : (3 + half) * HDIM, :] = got[HDIM:]
        tok3 = tok + half * 1024 - off3
        far = far + dot(kv[:HDIM], onehot(tok3 == lane * D3))
        far = far + dot(kv[HDIM:], onehot(tok3 == (lane - 64) * D3))
    kv_ref[4 * HDIM :, :] = far.astype(BF)
    all_ref[...] = x_ref[:, HDIM:, :]


def near_kernel(seg, off_ref, x_ref, other_ref, state_ref, q_ref):
    core = lax.rem(lax.axis_index("seq"), 2)
    ones = jnp.ones((16, 256), BF)
    row = iota((256, 256), 0)
    col = iota((256, 256), 1)
    first = col < 128
    last = jnp.where(row < 128, lax.rem(col, 128), 127 + 128 * core)
    diagonal = (row <= jnp.where(first, last, 255), row <= jnp.where(first, -1, last))
    begin = 8 * seg
    for slot in range(begin, begin + 8, 2):
        q_t = jnp.concatenate([x_ref[slot + s, :HDIM, :] for s in range(2)], axis=1)
        parts = []
        for k_slot in range(begin, slot + 2):
            k_t = jnp.concatenate(
                [x_ref[k_slot, HDIM : 2 * HDIM, :], other_ref[k_slot, :HDIM, :]], axis=1
            )
            scores = contract0(k_t, q_t)
            if k_slot >= slot:
                scores = jnp.where(diagonal[k_slot - slot], scores, LOW)
            parts.append(scores)
        high = functools.reduce(
            jnp.maximum, [jnp.max(p, axis=0, keepdims=True) for p in parts]
        ) * SCALE
        acc = jnp.zeros((AUG, 256), F32)
        for k_slot, scores in zip(range(begin, slot + 2), parts):
            v_t = jnp.concatenate(
                [x_ref[k_slot, 2 * HDIM : 3 * HDIM, :], other_ref[k_slot, HDIM:, :]], axis=1
            )
            weights = jnp.exp2(scores * SCALE - high).astype(BF)
            acc = acc + dot(jnp.concatenate([v_t, ones], axis=0), weights)
        cols = slice((slot - begin) * 128, (slot - begin + 2) * 128)
        state_ref[:ROW_M, cols] = acc[:ROW_M]
        state_ref[ROW_M:, cols] = jnp.broadcast_to(high, (8, 256))
    off2, off3 = my_offsets(off_ref)
    tok = iota((1024, 128), 0)
    lane = iota((1024, 128), 1)
    q_t = blocks(x_ref, begin, 0, HDIM)
    q_ref[:HDIM, :] = dot(q_t, onehot(tok == lane * D2 + off2)).astype(BF)
    q_ref[HDIM:, :] = dot(q_t, onehot(tok + seg * 1024 == lane * D3 + off3)).astype(BF)


def stack_kernel(a_ref, b_ref, c_ref, d_ref, after_ref, out_ref):
    del after_ref
    for n, ref in enumerate((a_ref, b_ref, c_ref, d_ref)):
        out_ref[n] = ref[...]


def split3(x):
    top = x.astype(BF)
    rest = x - top.astype(F32)
    mid = rest.astype(BF)
    return top, mid, (rest - mid.astype(F32)).astype(BF)


def spread(acc, high, place):
    top, mid, _ = split3(acc[:HDIM])
    stat = jnp.concatenate(
        [acc[ROW_L : ROW_L + 8], jnp.broadcast_to(high, (8, high.shape[1]))], axis=0
    )
    stats = split3(stat)
    out = dot(jnp.concatenate((top, mid) + stats, axis=0), place)
    base = 2 * HDIM
    stat = out[base : base + 16] + out[base + 16 : base + 32] + out[base + 32 : base + 48]
    return out[:HDIM] + out[HDIM : 2 * HDIM], stat[:1], stat[8:9]


def far_kernel(off_ref, state0_ref, state1_ref, q0_ref, q1_ref, own_ref, other_ref, out_ref):
    pieces = [ref.at[n] for n in range(4) for ref in (own_ref, other_ref)]
    off2, off3 = my_offsets(off_ref)
    device = lax.axis_index("seq")
    core = lax.rem(device, 2)
    plane = device // 32

    def hide(scores, n, row, col, slot_rows):
        if n == 0:
            return jnp.where(row <= col, scores, LOW)
        if n == 1:
            return jnp.where(row // slot_rows < col // slot_rows + core, scores, LOW)
        return jnp.where(plane >= n // 2, scores, LOW)

    q2 = jnp.concatenate([q0_ref[:HDIM, :], q1_ref[:HDIM, :]], axis=1)
    row = iota((C2, C2), 0)
    col = iota((C2, C2), 1)
    parts = []
    for n, piece in enumerate(pieces):
        k_t = jnp.concatenate([piece[:HDIM, :], piece[HDIM : 2 * HDIM, :]], axis=1)
        parts.append(hide(contract0(k_t, q2), n, row, col, ROWS // D2))
    high2 = functools.reduce(
        jnp.maximum, [jnp.max(p, axis=0, keepdims=True) for p in parts]
    ) * SCALE
    acc2 = jnp.zeros((AUG, C2), F32)
    ones = jnp.ones((16, C2), BF)
    for piece, scores in zip(pieces, parts):
        v_t = jnp.concatenate(
            [piece[2 * HDIM : 3 * HDIM, :], piece[3 * HDIM : 4 * HDIM, :]], axis=1
        )
        weights = jnp.exp2(scores * SCALE - high2).astype(BF)
        acc2 = acc2 + dot(jnp.concatenate([v_t, ones], axis=0), weights)
    q3 = q0_ref[HDIM:, :] + q1_ref[HDIM:, :]
    row = iota((C3, 128), 0)
    col = iota((C3, 128), 1)
    parts = []
    for n, piece in enumerate(pieces):
        scores = contract0(piece[4 * HDIM :, :], q3)[:C3]
        parts.append(hide(scores, n, row, col, ROWS // D3))
    high3 = functools.reduce(
        jnp.maximum, [jnp.max(p, axis=0, keepdims=True) for p in parts]
    ) * SCALE
    acc3 = jnp.zeros((AUG, 128), F32)
    ones = jnp.ones((16, 128), BF)
    for piece, scores in zip(pieces, parts):
        weights = jnp.exp2(scores * SCALE - high3).astype(BF)
        weights = jnp.concatenate([jnp.zeros((C3, 128), BF), weights], axis=0)
        acc3 = acc3 + dot(jnp.concatenate([piece[4 * HDIM :, :], ones], axis=0), weights)
    lane = iota((128, 1024), 0)
    tok = iota((128, 1024), 1)
    place2 = onehot(tok == lane * D2 + off2)
    tok1 = iota((1, 1024), 1)
    for half in range(2):
        near = (state0_ref, state1_ref)[half][...]
        part = slice(half * 128, (half + 1) * 128)
        sum2, tot2, hi2 = spread(acc2[:, part], high2[:, part], place2)
        place3 = onehot(tok + half * 1024 == lane * D3 + off3)
        sum3, tot3, hi3 = spread(acc3, high3, place3)
        hi1 = near[ROW_M : ROW_M + 1]
        hi2 = jnp.where(lax.rem(tok1, D2) == off2, hi2, LOW)
        hi3 = jnp.where(lax.rem(tok1, D3) == off3, hi3, LOW)
        peak = jnp.maximum(jnp.maximum(hi1, hi2), hi3)
        e1, e2, e3 = jnp.exp2(hi1 - peak), jnp.exp2(hi2 - peak), jnp.exp2(hi3 - peak)
        inv = 1.0 / (e1 * near[ROW_L : ROW_L + 1] + e2 * tot2 + e3 * tot3)
        mixed = near[:HDIM] * (e1 * inv) + sum2 * (e2 * inv) + sum3 * (e3 * inv)
        mixed = mixed.astype(BF)
        for s in range(8):
            out_ref[half * 8 + s] = mixed[:, s * 128 : (s + 1) * 128]


def project_kernel(x_ref, w_ref, out_ref):
    x = jnp.concatenate([x_ref[h] for h in range(HEADS)], axis=0)
    out_ref[...] = contract0(x, w_ref[...]).astype(BF)


def call(kernel, out_shapes, smem, vmem, hbm=0, scratch=(), cost=None, limit=40):
    return pl.pallas_call(
        kernel,
        out_shape=out_shapes,
        in_specs=[pl.BlockSpec(memory_space=pltpu.SMEM)] * smem
        + [pl.BlockSpec(memory_space=pltpu.VMEM)] * vmem
        + [pl.BlockSpec(memory_space=pltpu.HBM)] * hbm,
        out_specs=jax.tree.map(lambda _: pl.BlockSpec(memory_space=pltpu.VMEM), out_shapes),
        scratch_shapes=scratch,
        cost_estimate=cost,
        compiler_params=pltpu.CompilerParams(vmem_limit_bytes=limit * 2**20),
    )


def shape(*dims, dtype=BF):
    return jax.ShapeDtypeStruct(dims, dtype)


def on_device(queries, key_states, value_states, offsets, out_weight):
    n_dev = 128
    planes = [[x * 32 + 2 * j + c for j in range(HEADS)] for x in range(4) for c in range(2)]
    swap = [(i, i ^ 1) for i in range(n_dev)]
    packed = call(
        pack_kernel,
        shape(HEADS, 3 * HDIM, ROWS),
        0,
        0,
        3,
        (pltpu.VMEM((3, ROWS, HEADS * HDIM), BF), pltpu.SemaphoreType.DMA((6,))),
        limit=60,
    )(queries, key_states, value_states)
    mine = lax.all_to_all(packed, "seq", 0, 0, axis_index_groups=planes, tiled=True)
    chosen, own_kv = call(
        select_kernel, (shape(5 * HDIM, 128), shape(HEADS, 2 * HDIM, ROWS)), 1, 1
    )(offsets, mine)
    other_kv = lax.ppermute(own_kv, "seq", swap)
    pieces = [chosen]
    for back in (1, 2, 3):
        pairs = [(i, (i + 32 * back) % n_dev) for i in range(n_dev)]
        pieces.append(lax.ppermute(chosen, "seq", pairs))
    near = [
        call(
            functools.partial(near_kernel, seg),
            (shape(AUG, SEG1 // 2, dtype=F32), shape(2 * HDIM, 128)),
            1,
            2,
            cost=pl.CostEstimate(flops=3 * 10**9, bytes_accessed=10**7, transcendentals=10**6),
        )
        for seg in range(2)
    ]
    state0, q0 = near[0](offsets, mine, other_kv)
    own = call(stack_kernel, shape(4, 5 * HDIM, 128), 0, 5)(*pieces, q0)
    other = lax.ppermute(own, "seq", swap)
    state1, q1 = near[1](offsets, mine, other_kv)
    mixed = call(far_kernel, shape(HEADS, HDIM, ROWS), 1, 6)(
        offsets, state0, state1, q0, q1, own, other
    )
    home = lax.all_to_all(mixed, "seq", 0, 0, axis_index_groups=planes, tiled=True)
    return call(project_kernel, shape(ROWS, HEADS * HDIM), 0, 2)(home, out_weight)


def solution(mesh):
    placed = (P("seq", None), P("seq", None), P("seq", None), P(), P())
    return jax.shard_map(
        on_device, mesh=mesh, in_specs=placed, out_specs=P("seq", None), check_vma=False
    )
```

```python
import functools
import math

import jax
import jax.numpy as jnp
from jax import lax
from jax.experimental import pallas as pl
from jax.experimental.pallas import tpu as pltpu
from jax.sharding import PartitionSpec as P

HEADS = 16
HDIM = 80
SEG1 = 2048
SEGS = 8
ROWS = 128
D2 = 8
D3 = 32
C2 = SEG1 // D2
C3 = SEG1 // D3
ROW_L = HDIM
ROW_M = HDIM + 8
AUG = HDIM + 16
SCALE = math.log2(math.e) / math.sqrt(HDIM)
LOW = -1e30
BF = jnp.bfloat16
F32 = jnp.float32


def contract0(a, b):
    return lax.dot_general(a, b, (((0,), (0,)), ((), ())), preferred_element_type=F32)


def dot(a, b):
    return jnp.dot(a, b, preferred_element_type=F32)


def iota(shape, dim):
    return lax.broadcasted_iota(jnp.int32, shape, dim)


def onehot(cond):
    return jnp.where(cond, 1.0, 0.0).astype(BF)


def my_offsets(off_ref):
    head = lax.rem(lax.axis_index("seq") // 2, HEADS)
    return off_ref[0, head], off_ref[1, head]


def blocks(ref, first, low, high):
    return jnp.concatenate([ref[s, low:high, :] for s in range(first, first + 8)], axis=1)


def pack_kernel(q_hbm, k_hbm, v_hbm, out_ref, held, sems):
    copies = [
        pltpu.make_async_copy(ref, held.at[part], sems.at[part])
        for part, ref in enumerate((q_hbm, k_hbm, v_hbm))
    ]
    for copy in copies:
        copy.start()
    half = HEADS * HDIM // 2
    for part in range(3):
        copies[part].wait()
        for n in range(2):
            turned = held[part, :, n * half : (n + 1) * half].T
            for m in range(8):
                out_ref[8 * n + m, part * HDIM : (part + 1) * HDIM, :] = turned[
                    m * HDIM : (m + 1) * HDIM
                ]


def select_kernel(off_ref, x_ref, kv_ref, all_ref):
    off2, off3 = my_offsets(off_ref)
    tok = iota((1024, 128), 0)
    lane = iota((1024, 128), 1)
    pick2 = onehot(tok == lane * D2 + off2)
    far = jnp.zeros((HDIM, 128), F32)
    for half in range(2):
        kv = blocks(x_ref, 8 * half, HDIM, 3 * HDIM)
        got = dot(kv, pick2).astype(BF)
        kv_ref[half * HDIM : (half + 1) * HDIM, :] = got[:HDIM]
        kv_ref[(2 + half) * HDIM : (3 + half) * HDIM, :] = got[HDIM:]
        tok3 = tok + half * 1024 - off3
        far = far + dot(kv[:HDIM], onehot(tok3 == lane * D3))
        far = far + dot(kv[HDIM:], onehot(tok3 == (lane - 64) * D3))
    kv_ref[4 * HDIM :, :] = far.astype(BF)
    all_ref[...] = x_ref[:, HDIM:, :]


def near_kernel(seg, off_ref, x_ref, other_ref, state_ref, q_ref):
    core = lax.rem(lax.axis_index("seq"), 2)
    ones = jnp.ones((16, 256), BF)
    row = iota((256, 256), 0)
    col = iota((256, 256), 1)
    first = col < 128
    last = jnp.where(row < 128, lax.rem(col, 128), 127 + 128 * core)
    diagonal = (row <= jnp.where(first, last, 255), row <= jnp.where(first, -1, last))
    begin = 8 * seg
    for slot in range(begin, begin + 8, 2):
        q_t = jnp.concatenate([x_ref[slot + s, :HDIM, :] for s in range(2)], axis=1)
        parts = []
        for k_slot in range(begin, slot + 2):
            k_t = jnp.concatenate(
                [x_ref[k_slot, HDIM : 2 * HDIM, :], other_ref[k_slot, :HDIM, :]], axis=1
            )
            scores = contract0(k_t, q_t)
            if k_slot >= slot:
                scores = jnp.where(diagonal[k_slot - slot], scores, LOW)
            parts.append(scores)
        high = functools.reduce(
            jnp.maximum, [jnp.max(p, axis=0, keepdims=True) for p in parts]
        ) * SCALE
        acc = jnp.zeros((AUG, 256), F32)
        for k_slot, scores in zip(range(begin, slot + 2), parts):
            v_t = jnp.concatenate(
                [x_ref[k_slot, 2 * HDIM : 3 * HDIM, :], other_ref[k_slot, HDIM:, :]], axis=1
            )
            weights = jnp.exp2(scores * SCALE - high).astype(BF)
            acc = acc + dot(jnp.concatenate([v_t, ones], axis=0), weights)
        cols = slice((slot - begin) * 128, (slot - begin + 2) * 128)
        state_ref[:ROW_M, cols] = acc[:ROW_M]
        state_ref[ROW_M:, cols] = jnp.broadcast_to(high, (8, 256))
    off2, off3 = my_offsets(off_ref)
    tok = iota((1024, 128), 0)
    lane = iota((1024, 128), 1)
    q_t = blocks(x_ref, begin, 0, HDIM)
    q_ref[:HDIM, :] = dot(q_t, onehot(tok == lane * D2 + off2)).astype(BF)
    q_ref[HDIM:, :] = dot(q_t, onehot(tok + seg * 1024 == lane * D3 + off3)).astype(BF)


def stack_kernel(a_ref, b_ref, c_ref, d_ref, after_ref, out_ref):
    del after_ref
    for n, ref in enumerate((a_ref, b_ref, c_ref, d_ref)):
        out_ref[n] = ref[...]


def split3(x):
    top = x.astype(BF)
    rest = x - top.astype(F32)
    mid = rest.astype(BF)
    return top, mid, (rest - mid.astype(F32)).astype(BF)


def spread(acc, high, place):
    top, mid, _ = split3(acc[:HDIM])
    stat = jnp.concatenate(
        [acc[ROW_L : ROW_L + 8], jnp.broadcast_to(high, (8, high.shape[1]))], axis=0
    )
    stats = split3(stat)
    out = dot(jnp.concatenate((top, mid) + stats, axis=0), place)
    base = 2 * HDIM
    stat = out[base : base + 16] + out[base + 16 : base + 32] + out[base + 32 : base + 48]
    return out[:HDIM] + out[HDIM : 2 * HDIM], stat[:1], stat[8:9]


def far_kernel(off_ref, state0_ref, state1_ref, q0_ref, q1_ref, own_ref, other_ref, out_ref):
    pieces = [ref.at[n] for n in range(4) for ref in (own_ref, other_ref)]
    off2, off3 = my_offsets(off_ref)
    device = lax.axis_index("seq")
    core = lax.rem(device, 2)
    plane = device // 32

    def hide(scores, n, row, col, slot_rows):
        if n == 0:
            return jnp.where(row <= col, scores, LOW)
        if n == 1:
            return jnp.where(row // slot_rows < col // slot_rows + core, scores, LOW)
        return jnp.where(plane >= n // 2, scores, LOW)

    q2 = jnp.concatenate([q0_ref[:HDIM, :], q1_ref[:HDIM, :]], axis=1)
    row = iota((C2, C2), 0)
    col = iota((C2, C2), 1)
    parts = []
    for n, piece in enumerate(pieces):
        k_t = jnp.concatenate([piece[:HDIM, :], piece[HDIM : 2 * HDIM, :]], axis=1)
        parts.append(hide(contract0(k_t, q2), n, row, col, ROWS // D2))
    high2 = functools.reduce(
        jnp.maximum, [jnp.max(p, axis=0, keepdims=True) for p in parts]
    ) * SCALE
    acc2 = jnp.zeros((AUG, C2), F32)
    ones = jnp.ones((16, C2), BF)
    for piece, scores in zip(pieces, parts):
        v_t = jnp.concatenate(
            [piece[2 * HDIM : 3 * HDIM, :], piece[3 * HDIM : 4 * HDIM, :]], axis=1
        )
        weights = jnp.exp2(scores * SCALE - high2).astype(BF)
        acc2 = acc2 + dot(jnp.concatenate([v_t, ones], axis=0), weights)
    q3 = q0_ref[HDIM:, :] + q1_ref[HDIM:, :]
    row = iota((C3, 128), 0)
    col = iota((C3, 128), 1)
    parts = []
    for n, piece in enumerate(pieces):
        scores = contract0(piece[4 * HDIM :, :], q3)[:C3]
        parts.append(hide(scores, n, row, col, ROWS // D3))
    high3 = functools.reduce(
        jnp.maximum, [jnp.max(p, axis=0, keepdims=True) for p in parts]
    ) * SCALE
    acc3 = jnp.zeros((AUG, 128), F32)
    ones = jnp.ones((16, 128), BF)
    for piece, scores in zip(pieces, parts):
        weights = jnp.exp2(scores * SCALE - high3).astype(BF)
        weights = jnp.concatenate([jnp.zeros((C3, 128), BF), weights], axis=0)
        acc3 = acc3 + dot(jnp.concatenate([piece[4 * HDIM :, :], ones], axis=0), weights)
    lane = iota((128, 1024), 0)
    tok = iota((128, 1024), 1)
    place2 = onehot(tok == lane * D2 + off2)
    tok1 = iota((1, 1024), 1)
    for half in range(2):
        near = (state0_ref, state1_ref)[half][...]
        part = slice(half * 128, (half + 1) * 128)
        sum2, tot2, hi2 = spread(acc2[:, part], high2[:, part], place2)
        place3 = onehot(tok + half * 1024 == lane * D3 + off3)
        sum3, tot3, hi3 = spread(acc3, high3, place3)
        hi1 = near[ROW_M : ROW_M + 1]
        hi2 = jnp.where(lax.rem(tok1, D2) == off2, hi2, LOW)
        hi3 = jnp.where(lax.rem(tok1, D3) == off3, hi3, LOW)
        peak = jnp.maximum(jnp.maximum(hi1, hi2), hi3)
        e1, e2, e3 = jnp.exp2(hi1 - peak), jnp.exp2(hi2 - peak), jnp.exp2(hi3 - peak)
        inv = 1.0 / (e1 * near[ROW_L : ROW_L + 1] + e2 * tot2 + e3 * tot3)
        mixed = near[:HDIM] * (e1 * inv) + sum2 * (e2 * inv) + sum3 * (e3 * inv)
        mixed = mixed.astype(BF)
        for s in range(8):
            out_ref[half * 8 + s] = mixed[:, s * 128 : (s + 1) * 128]


def project_kernel(x_ref, w_ref, out_ref):
    x = jnp.concatenate([x_ref[h] for h in range(HEADS)], axis=0)
    out_ref[...] = contract0(x, w_ref[...]).astype(BF)


def call(kernel, out_shapes, smem, vmem, hbm=0, scratch=(), cost=None):
    return pl.pallas_call(
        kernel,
        out_shape=out_shapes,
        in_specs=[pl.BlockSpec(memory_space=pltpu.SMEM)] * smem
        + [pl.BlockSpec(memory_space=pltpu.VMEM)] * vmem
        + [pl.BlockSpec(memory_space=pltpu.HBM)] * hbm,
        out_specs=jax.tree.map(lambda _: pl.BlockSpec(memory_space=pltpu.VMEM), out_shapes),
        scratch_shapes=scratch,
        cost_estimate=cost,
        compiler_params=pltpu.CompilerParams(vmem_limit_bytes=40 * 2**20),
    )


def shape(*dims, dtype=BF):
    return jax.ShapeDtypeStruct(dims, dtype)


def on_device(queries, key_states, value_states, offsets, out_weight):
    n_dev = 128
    planes = [[x * 32 + 2 * j + c for j in range(HEADS)] for x in range(4) for c in range(2)]
    swap = [(i, i ^ 1) for i in range(n_dev)]
    packed = call(
        pack_kernel,
        shape(HEADS, 3 * HDIM, ROWS),
        0,
        0,
        3,
        (pltpu.VMEM((3, ROWS, HEADS * HDIM), BF), pltpu.SemaphoreType.DMA((3,))),
    )(*[pltpu.with_memory_space_constraint(a, pltpu.HBM) for a in (queries, key_states, value_states)])
    mine = lax.all_to_all(packed, "seq", 0, 0, axis_index_groups=planes, tiled=True)
    chosen, own_kv = call(
        select_kernel, (shape(5 * HDIM, 128), shape(HEADS, 2 * HDIM, ROWS)), 1, 1
    )(offsets, mine)
    other_kv = lax.ppermute(own_kv, "seq", swap)
    pieces = [chosen]
    for back in (1, 2, 3):
        pairs = [(i, (i + 32 * back) % n_dev) for i in range(n_dev)]
        pieces.append(lax.ppermute(chosen, "seq", pairs))
    near = [
        call(
            functools.partial(near_kernel, seg),
            (shape(AUG, SEG1 // 2, dtype=F32), shape(2 * HDIM, 128)),
            1,
            2,
            cost=pl.CostEstimate(flops=3 * 10**9, bytes_accessed=10**7, transcendentals=10**6),
        )
        for seg in range(2)
    ]
    state0, q0 = near[0](offsets, mine, other_kv)
    own = call(stack_kernel, shape(4, 5 * HDIM, 128), 0, 5)(*pieces, q0)
    other = lax.ppermute(own, "seq", swap)
    state1, q1 = near[1](offsets, mine, other_kv)
    mixed = call(far_kernel, shape(HEADS, HDIM, ROWS), 1, 6)(
        offsets, state0, state1, q0, q1, own, other
    )
    home = lax.all_to_all(mixed, "seq", 0, 0, axis_index_groups=planes, tiled=True)
    return call(project_kernel, shape(ROWS, HEADS * HDIM), 0, 2)(home, out_weight)


def solution(mesh):
    placed = (P("seq", None), P("seq", None), P("seq", None), P(), P())
    return jax.shard_map(
        on_device, mesh=mesh, in_specs=placed, out_specs=P("seq", None), check_vma=False
    )
```

```python
import functools
import math

import jax
import jax.numpy as jnp
from jax import lax
from jax.experimental import pallas as pl
from jax.experimental.pallas import tpu as pltpu
from jax.sharding import PartitionSpec as P

HEADS = 16
HDIM = 80
SEG1 = 2048
SEGS = 8
ROWS = 128
D2 = 8
D3 = 32
C2 = SEG1 // D2
C3 = SEG1 // D3
ROW_L = HDIM
ROW_M = HDIM + 8
AUG = HDIM + 16
SCALE = math.log2(math.e) / math.sqrt(HDIM)
LOW = -1e30
BF = jnp.bfloat16
F32 = jnp.float32


def contract0(a, b):
    return lax.dot_general(a, b, (((0,), (0,)), ((), ())), preferred_element_type=F32)


def dot(a, b):
    return jnp.dot(a, b, preferred_element_type=F32)


def iota(shape, dim):
    return lax.broadcasted_iota(jnp.int32, shape, dim)


def onehot(cond):
    return jnp.where(cond, 1.0, 0.0).astype(BF)


def my_offsets(off_ref):
    head = lax.rem(lax.axis_index("seq") // 2, HEADS)
    mine = jnp.where(iota((2, HEADS), 1) == head, off_ref[...], 0)
    both = jnp.sum(mine, axis=1, keepdims=True)
    return both[:1], both[1:]


def picks(off_ref, first):
    off2, off3 = my_offsets(off_ref)
    tok = iota((1024, 128), 0)
    lane = iota((1024, 128), 1)
    return jnp.concatenate(
        [onehot(tok == lane * D2 + off2), onehot(tok + first * 128 == lane * D3 + off3)], axis=1
    )


def fold(x):
    return jnp.max(x.reshape(x.shape[0] // 8, 8, x.shape[1]), axis=0)


def blocks(ref, first, low, high):
    return jnp.concatenate([ref[s, low:high, :] for s in range(first, first + 8)], axis=1)


def pack_kernel(q_hbm, k_hbm, v_hbm, out_ref, held, sems):
    copies = [
        pltpu.make_async_copy(ref, held.at[part], sems.at[part])
        for part, ref in enumerate((q_hbm, k_hbm, v_hbm))
    ]
    for copy in copies:
        copy.start()
    half = HEADS * HDIM // 2
    for part in range(3):
        copies[part].wait()
        for n in range(2):
            turned = held[part, :, n * half : (n + 1) * half].T
            for m in range(8):
                out_ref[8 * n + m, part * HDIM : (part + 1) * HDIM, :] = turned[
                    m * HDIM : (m + 1) * HDIM
                ]


def select_kernel(off_ref, x_ref, kv_ref, all_ref):
    kv = jnp.concatenate([blocks(x_ref, 8 * h, HDIM, 3 * HDIM) for h in range(2)], axis=0)
    got = dot(kv, picks(off_ref, 0))
    key0, val0, key1, val1 = [got[n * HDIM : (n + 1) * HDIM] for n in range(4)]
    for n, part in enumerate((key0, key1, val0, val1)):
        kv_ref[n * HDIM : (n + 1) * HDIM, :] = part[:, :128].astype(BF)
    far = key0[:, 128:]
    for n, part in enumerate((key1, val0, val1)):
        far = far + pltpu.roll(part[:, 128:], 32 * (n + 1), 1)
    kv_ref[4 * HDIM :, :] = far.astype(BF)
    all_ref[...] = x_ref[:, HDIM:, :]


def near_kernel(seg, off_ref, x_ref, other_ref, state_ref, q_ref):
    core = lax.rem(lax.axis_index("seq"), 2)
    ones = jnp.ones((16, 256), BF)
    row = iota((256, 256), 0)
    col = iota((256, 256), 1)
    first = col < 128
    last = jnp.where(row < 128, lax.rem(col, 128), 127 + 128 * core)
    diagonal = (row <= jnp.where(first, last, 255), row <= jnp.where(first, -1, last))
    begin = 8 * seg
    keys = [
        jnp.concatenate([x_ref[s, HDIM : 2 * HDIM, :], other_ref[s, :HDIM, :]], axis=1).T
        for s in range(begin, begin + 8)
    ]

    def score(slot):
        q_t = jnp.concatenate([x_ref[begin + slot + n, :HDIM, :] for n in range(2)], axis=1)
        parts = [dot(keys[n], q_t) for n in range(slot + 2)]
        for n in range(2):
            parts[slot + n] = jnp.where(diagonal[n], parts[slot + n], LOW)
        return parts

    def weigh(parts):
        top = functools.reduce(jnp.maximum, [fold(p) for p in parts])
        high = jnp.max(top, axis=0, keepdims=True) * SCALE
        return high, [jnp.exp2(p * SCALE - high).astype(BF) for p in parts]

    def gather(slot, high, weights):
        acc = jnp.zeros((AUG, 256), F32)
        for n, part in enumerate(weights):
            s = begin + n
            v_t = jnp.concatenate([x_ref[s, 2 * HDIM :, :], other_ref[s, HDIM:, :]], axis=1)
            acc = acc + dot(jnp.concatenate([v_t, ones], axis=0), part)
        cols = slice(slot * 128, (slot + 2) * 128)
        state_ref[:ROW_M, cols] = acc[:ROW_M]
        state_ref[ROW_M:, cols] = jnp.broadcast_to(high, (8, 256))

    order = (6, 4, 2, 0)
    scores = score(order[0])
    waiting = None
    for n, slot in enumerate(order):
        current = scores
        if n + 1 < len(order):
            scores = score(order[n + 1])
        weighed = weigh(current)
        if waiting is not None:
            gather(*waiting)
        waiting = (slot, *weighed)
    gather(*waiting)
    got = dot(blocks(x_ref, begin, 0, HDIM), picks(off_ref, begin))
    q_ref[:HDIM, :] = got[:, :128].astype(BF)
    q_ref[HDIM:, :] = got[:, 128:].astype(BF)


def stack_kernel(a_ref, b_ref, c_ref, d_ref, after_ref, out_ref):
    del after_ref
    for n, ref in enumerate((a_ref, b_ref, c_ref, d_ref)):
        out_ref[n] = ref[...]


def far_kernel(off_ref, state0_ref, state1_ref, q0_ref, q1_ref, own_ref, other_ref, out_ref):
    pieces = [ref.at[n] for n in range(4) for ref in (own_ref, other_ref)]
    off2, off3 = my_offsets(off_ref)
    device = lax.axis_index("seq")
    core = lax.rem(device, 2)
    plane = device // 32

    def attend(width, keys, values, q, slot_rows):
        row = iota((width, q.shape[1]), 0)
        col = iota((width, q.shape[1]), 1)
        parts, tops, hides = [], [], []
        for n, k_t in enumerate(keys):
            scores = contract0(k_t, q)[:width]
            if n == 0:
                scores = jnp.where(row <= col, scores, LOW)
            if n == 1:
                scores = jnp.where(row // slot_rows < col // slot_rows + core, scores, LOW)
            hide = jnp.where(plane >= n // 2, 0.0, LOW).astype(F32)
            parts.append(scores)
            hides.append(hide)
            tops.append(fold(scores) + hide)
        high = jnp.max(functools.reduce(jnp.maximum, tops), axis=0, keepdims=True) * SCALE
        high = high.astype(BF).astype(F32)
        acc = jnp.zeros((AUG, q.shape[1]), F32)
        for v_t, scores, hide in zip(values, parts, hides):
            weights = jnp.exp2(scores * SCALE - (high - hide)).astype(BF)
            if v_t.shape[1] > width:
                zeros = jnp.zeros((v_t.shape[1] - width, q.shape[1]), BF)
                weights = jnp.concatenate([zeros, weights], axis=0)
            ones = jnp.ones((16, v_t.shape[1]), BF)
            acc = acc + dot(jnp.concatenate([v_t, ones], axis=0), weights)
        body = acc[:ROW_M]
        top = body.astype(BF)
        rest = (body - top.astype(F32)).astype(BF)
        stat = jnp.broadcast_to(high, (8, q.shape[1])).astype(BF)
        return (
            jnp.concatenate([top, stat], axis=0),
            jnp.concatenate([rest, jnp.zeros_like(stat)], axis=0),
        )

    def pair(piece, n):
        return jnp.concatenate(
            [piece[n * HDIM : (n + 1) * HDIM, :], piece[(n + 1) * HDIM : (n + 2) * HDIM, :]], axis=1
        )

    q2 = jnp.concatenate([q0_ref[:HDIM, :], q1_ref[:HDIM, :]], axis=1)
    top2, rest2 = attend(
        C2, [pair(p, 0) for p in pieces], [pair(p, 2) for p in pieces], q2, ROWS // D2
    )
    q3 = q0_ref[HDIM:, :] + q1_ref[HDIM:, :]
    last = [p[4 * HDIM :, :] for p in pieces]
    parts3 = jnp.concatenate(attend(C3, last, last, q3, ROWS // D3), axis=1)
    lane = iota((128, 1024), 0)
    tok = iota((128, 1024), 1)
    place2 = onehot(tok == lane * D2 + off2)
    place2 = jnp.concatenate([place2, place2], axis=0)
    tok1 = iota((1, 1024), 1)
    for half in range(2):
        near = (state0_ref, state1_ref)[half][...]
        cols = slice(half * 128, (half + 1) * 128)
        lev2 = dot(jnp.concatenate([top2[:, cols], rest2[:, cols]], axis=1), place2)
        place3 = onehot(tok + half * 1024 == lane * D3 + off3)
        lev3 = dot(parts3, jnp.concatenate([place3, place3], axis=0))
        hi1 = near[ROW_M : ROW_M + 1]
        hi2 = jnp.where(lax.rem(tok1, D2) == off2, lev2[ROW_M : ROW_M + 1], LOW)
        hi3 = jnp.where(lax.rem(tok1, D3) == off3, lev3[ROW_M : ROW_M + 1], LOW)
        peak = jnp.maximum(jnp.maximum(hi1, hi2), hi3)
        shares = [jnp.exp2(hi - peak) for hi in (hi1, hi2, hi3)]
        levels = (near, lev2, lev3)
        total = sum(e * x[ROW_L : ROW_L + 1] for e, x in zip(shares, levels))
        inv = 1.0 / total
        mixed = sum(x[:HDIM] * (e * inv) for e, x in zip(shares, levels)).astype(BF)
        for s in range(8):
            out_ref[half * 8 + s] = mixed[:, s * 128 : (s + 1) * 128]


def project_kernel(x_ref, w_ref, out_ref):
    x = jnp.concatenate([x_ref[h] for h in range(HEADS)], axis=0)
    out_ref[...] = contract0(x, w_ref[...]).astype(BF)


def call(kernel, out_shapes, vmem, hbm=0, scratch=(), cost=None):
    return pl.pallas_call(
        kernel,
        out_shape=out_shapes,
        in_specs=[pl.BlockSpec(memory_space=pltpu.VMEM)] * vmem
        + [pl.BlockSpec(memory_space=pltpu.HBM)] * hbm,
        out_specs=jax.tree.map(lambda _: pl.BlockSpec(memory_space=pltpu.VMEM), out_shapes),
        scratch_shapes=scratch,
        cost_estimate=cost,
        compiler_params=pltpu.CompilerParams(vmem_limit_bytes=40 * 2**20),
    )


def shape(*dims, dtype=BF):
    return jax.ShapeDtypeStruct(dims, dtype)


def on_device(queries, key_states, value_states, offsets, out_weight):
    n_dev = 128
    planes = [[x * 32 + 2 * j + c for j in range(HEADS)] for x in range(4) for c in range(2)]
    swap = [(i, i ^ 1) for i in range(n_dev)]
    packed = call(
        pack_kernel,
        shape(HEADS, 3 * HDIM, ROWS),
        0,
        3,
        (pltpu.VMEM((3, ROWS, HEADS * HDIM), BF), pltpu.SemaphoreType.DMA((3,))),
    )(*[pltpu.with_memory_space_constraint(a, pltpu.HBM) for a in (queries, key_states, value_states)])
    mine = lax.all_to_all(packed, "seq", 0, 0, axis_index_groups=planes, tiled=True)
    chosen, own_kv = call(
        select_kernel, (shape(5 * HDIM, 128), shape(HEADS, 2 * HDIM, ROWS)), 2
    )(offsets, mine)
    other_kv = lax.ppermute(own_kv, "seq", swap)
    pieces = [chosen]
    for back in (1, 2, 3):
        pairs = [(i, (i + 32 * back) % n_dev) for i in range(n_dev)]
        pieces.append(lax.ppermute(chosen, "seq", pairs))
    near = [
        call(
            functools.partial(near_kernel, seg),
            (shape(AUG, SEG1 // 2, dtype=F32), shape(2 * HDIM, 128)),
            3,
            cost=pl.CostEstimate(flops=3 * 10**9, bytes_accessed=10**7, transcendentals=10**6),
        )
        for seg in range(2)
    ]
    state0, q0 = near[0](offsets, mine, other_kv)
    own = call(stack_kernel, shape(4, 5 * HDIM, 128), 5)(*pieces, q0)
    other = lax.ppermute(own, "seq", swap)
    state1, q1 = near[1](offsets, mine, other_kv)
    mixed = call(far_kernel, shape(HEADS, HDIM, ROWS), 7)(
        offsets, state0, state1, q0, q1, own, other
    )
    home = lax.all_to_all(mixed, "seq", 0, 0, axis_index_groups=planes, tiled=True)
    return call(project_kernel, shape(ROWS, HEADS * HDIM), 2)(home, out_weight)


def solution(mesh):
    placed = (P("seq", None), P("seq", None), P("seq", None), P(), P())
    return jax.shard_map(
        on_device, mesh=mesh, in_specs=placed, out_specs=P("seq", None), check_vma=False
    )
```

```python
import functools
import math

import jax
import jax.numpy as jnp
from jax import lax
from jax.experimental import pallas as pl
from jax.experimental.pallas import tpu as pltpu
from jax.sharding import PartitionSpec as P

HEADS = 16
HDIM = 80
SEG1 = 2048
SEGS = 8
ROWS = 128
D2 = 8
D3 = 32
C2 = SEG1 // D2
C3 = SEG1 // D3
ROW_L = HDIM
ROW_M = HDIM + 8
AUG = HDIM + 16
SCALE = math.log2(math.e) / math.sqrt(HDIM)
LOW = -1e30
FLOOR = -1e9
BF = jnp.bfloat16
F32 = jnp.float32


def contract0(a, b):
    return lax.dot_general(a, b, (((0,), (0,)), ((), ())), preferred_element_type=F32)


def dot(a, b):
    return jnp.dot(a, b, preferred_element_type=F32)


def iota(shape, dim):
    return lax.broadcasted_iota(jnp.int32, shape, dim)


def onehot(cond):
    return jnp.where(cond, 1.0, 0.0).astype(BF)


def my_offsets(off_ref):
    head = lax.rem(lax.axis_index("seq") // 2, HEADS)
    mine = jnp.where(iota((2, HEADS), 1) == head, off_ref[...], 0)
    both = jnp.sum(mine, axis=1, keepdims=True)
    return both[:1], both[1:]


def picks(off_ref):
    off2, off3 = my_offsets(off_ref)
    tok = iota((1024, 128), 0)
    lane = iota((1024, 128), 1)
    return jnp.concatenate(
        [onehot(tok == lane * D2 + off2), onehot(tok == lane * D3 + off3)], axis=1
    )


def fold(x):
    return jnp.max(x.reshape(x.shape[0] // 8, 8, x.shape[1]), axis=0)


def blocks(ref, first, low, high):
    return jnp.concatenate([ref[s, low:high, :] for s in range(first, first + 8)], axis=1)


def pack_kernel(q_hbm, k_hbm, v_hbm, out_ref, held, sems):
    copies = [
        pltpu.make_async_copy(ref, held.at[part], sems.at[part])
        for part, ref in enumerate((q_hbm, k_hbm, v_hbm))
    ]
    for copy in copies:
        copy.start()
    half = HEADS * HDIM // 2
    for part in range(3):
        copies[part].wait()
        for n in range(2):
            turned = held[part, :, n * half : (n + 1) * half].T
            for m in range(8):
                out_ref[8 * n + m, part * HDIM : (part + 1) * HDIM, :] = turned[
                    m * HDIM : (m + 1) * HDIM
                ]


def select_kernel(off_ref, x_ref, kv_ref, q_ref, all_ref):
    both = jnp.concatenate([blocks(x_ref, 8 * h, 0, 3 * HDIM) for h in range(2)], axis=0)
    got = dot(both, picks(off_ref))
    q0, key0, val0, q1, key1, val1 = [got[n * HDIM : (n + 1) * HDIM] for n in range(6)]
    for n, part in enumerate((key0, key1, val0, val1)):
        kv_ref[n * HDIM : (n + 1) * HDIM, :] = part[:, :128].astype(BF)
    far = key0[:, 128:]
    for n, part in enumerate((key1, val0, val1)):
        far = far + pltpu.roll(part[:, 128:], 32 * (n + 1), 1)
    kv_ref[4 * HDIM :, :] = far.astype(BF)
    q_ref[:, :128] = q0[:, :128].astype(BF)
    q_ref[:, 128:256] = q1[:, :128].astype(BF)
    q_ref[:, 256:] = (q0[:, 128:] + pltpu.roll(q1[:, 128:], 32, 1)).astype(BF)
    all_ref[...] = x_ref[:, HDIM:, :]


def near_kernel(x_ref, other_ref, state_ref):
    core = lax.rem(lax.axis_index("seq"), 2)
    ones = jnp.ones((16, 256), BF)
    row = iota((256, 256), 0)
    col = iota((256, 256), 1)
    first = col < 128
    last = jnp.where(row < 128, lax.rem(col, 128), 127 + 128 * core)
    diagonal = (row <= jnp.where(first, last, 255), row <= jnp.where(first, -1, last))
    keys = [
        jnp.concatenate([x_ref[s, HDIM : 2 * HDIM, :], other_ref[s, :HDIM, :]], axis=1).T
        for s in range(HEADS)
    ]

    def score(slot):
        q_t = jnp.concatenate([x_ref[slot + n, :HDIM, :] for n in range(2)], axis=1)
        parts = [dot(keys[n], q_t) for n in range(slot // 8 * 8, slot + 2)]
        for n in range(2):
            parts[n - 2] = jnp.where(diagonal[n], parts[n - 2], LOW)
        return parts

    def weigh(parts):
        top = functools.reduce(jnp.maximum, [fold(p) for p in parts])
        high = jnp.max(top, axis=0, keepdims=True) * SCALE
        return high, [jnp.exp2(p * SCALE - high).astype(BF) for p in parts]

    def gather(slot, high, weights):
        acc = jnp.zeros((AUG, 256), F32)
        for n, part in enumerate(weights):
            s = slot // 8 * 8 + n
            v_t = jnp.concatenate([x_ref[s, 2 * HDIM :, :], other_ref[s, HDIM:, :]], axis=1)
            acc = acc + dot(jnp.concatenate([v_t, ones], axis=0), part)
        cols = slice(slot * 128, (slot + 2) * 128)
        state_ref[:ROW_M, cols] = acc[:ROW_M]
        state_ref[ROW_M:, cols] = jnp.broadcast_to(high, (8, 256))

    order = (6, 14, 4, 12, 2, 10, 0, 8)
    scores = score(order[0])
    waiting = None
    for n, slot in enumerate(order):
        current = scores
        if n + 1 < len(order):
            scores = score(order[n + 1])
        weighed = weigh(current)
        if waiting is not None:
            gather(*waiting)
        waiting = (slot, *weighed)
    gather(*waiting)


def far_kernel(own, q_ref, *refs):
    pieces, out_ref = refs[:4], refs[-1]
    device = lax.axis_index("seq")
    core = lax.rem(device, 2)
    plane = device // 32

    def attend(width, keys, values, q, slot_rows, cols):
        row = iota((width, q.shape[1]), 0)
        col = iota((width, q.shape[1]), 1)
        if own:
            seen = row <= col
        else:
            seen = row // slot_rows < col // slot_rows + 1 - core
        parts, tops, hides = [], [], []
        for n, k_t in enumerate(keys):
            scores = contract0(k_t, q)[:width]
            if n == 0:
                scores = jnp.where(seen, scores, LOW)
            hide = jnp.where(plane >= n, 0.0, LOW).astype(F32)
            parts.append(scores)
            hides.append(hide)
            tops.append(fold(scores) + hide)
        high = jnp.max(functools.reduce(jnp.maximum, tops), axis=0, keepdims=True) * SCALE
        high = jnp.maximum(high, FLOOR).astype(BF).astype(F32)
        acc = jnp.zeros((AUG, q.shape[1]), F32)
        for v_t, scores, hide in zip(values, parts, hides):
            weights = jnp.exp2(scores * SCALE - (high - hide)).astype(BF)
            if v_t.shape[1] > width:
                zeros = jnp.zeros((v_t.shape[1] - width, q.shape[1]), BF)
                weights = jnp.concatenate([zeros, weights], axis=0)
            ones = jnp.ones((16, v_t.shape[1]), BF)
            acc = acc + dot(jnp.concatenate([v_t, ones], axis=0), weights)
        out_ref[:ROW_M, cols] = acc[:ROW_M]
        out_ref[ROW_M:, cols] = jnp.broadcast_to(high, (8, q.shape[1]))

    def pair(piece, n):
        return jnp.concatenate(
            [piece[n * HDIM : (n + 1) * HDIM, :], piece[(n + 1) * HDIM : (n + 2) * HDIM, :]], axis=1
        )

    keys = [pair(p, 0) for p in pieces]
    values = [pair(p, 2) for p in pieces]
    last = [p[4 * HDIM :, :] for p in pieces]
    attend(C2, keys, values, q_ref[:, :C2], ROWS // D2, slice(0, C2))
    attend(C3, last, last, q_ref[:, C2:], ROWS // D3, slice(C2, C2 + 128))


def mix_kernel(off_ref, state_ref, own_ref, other_ref, out_ref):
    off2, off3 = my_offsets(off_ref)
    hi_a, hi_b = own_ref[ROW_M:, :], other_ref[ROW_M:, :]
    high = jnp.maximum(hi_a, hi_b)
    e_a, e_b = jnp.exp2(hi_a - high), jnp.exp2(hi_b - high)
    body = own_ref[:ROW_M, :] * e_a[:1] + other_ref[:ROW_M, :] * e_b[:1]
    top = body.astype(BF)
    rest = (body - top.astype(F32)).astype(BF)
    stat = high.astype(BF)
    top = jnp.concatenate([top, stat], axis=0)
    rest = jnp.concatenate([rest, jnp.zeros_like(stat)], axis=0)
    parts3 = jnp.concatenate([top[:, C2:], rest[:, C2:]], axis=1)
    lane = iota((128, 1024), 0)
    tok = iota((128, 1024), 1)
    place2 = onehot(tok == lane * D2 + off2)
    place2 = jnp.concatenate([place2, place2], axis=0)
    tok1 = iota((1, 1024), 1)
    for half in range(2):
        near = state_ref[:, half * 1024 : (half + 1) * 1024]
        cols = slice(half * 128, (half + 1) * 128)
        lev2 = dot(jnp.concatenate([top[:, cols], rest[:, cols]], axis=1), place2)
        place3 = onehot(tok + half * 1024 == lane * D3 + off3)
        lev3 = dot(parts3, jnp.concatenate([place3, place3], axis=0))
        hi1 = near[ROW_M : ROW_M + 1]
        hi2 = jnp.where(lax.rem(tok1, D2) == off2, lev2[ROW_M : ROW_M + 1], LOW)
        hi3 = jnp.where(lax.rem(tok1, D3) == off3, lev3[ROW_M : ROW_M + 1], LOW)
        peak = jnp.maximum(jnp.maximum(hi1, hi2), hi3)
        shares = [jnp.exp2(hi - peak) for hi in (hi1, hi2, hi3)]
        levels = (near, lev2, lev3)
        total = sum(e * x[ROW_L : ROW_L + 1] for e, x in zip(shares, levels))
        inv = 1.0 / total
        mixed = sum(x[:HDIM] * (e * inv) for e, x in zip(shares, levels)).astype(BF)
        for s in range(8):
            out_ref[half * 8 + s] = mixed[:, s * 128 : (s + 1) * 128]


def project_kernel(x_ref, w_ref, out_ref):
    x = jnp.concatenate([x_ref[h] for h in range(HEADS)], axis=0)
    out_ref[...] = contract0(x, w_ref[...]).astype(BF)


def call(kernel, out_shapes, vmem, hbm=0, scratch=(), cost=None):
    return pl.pallas_call(
        kernel,
        out_shape=out_shapes,
        in_specs=[pl.BlockSpec(memory_space=pltpu.VMEM)] * vmem
        + [pl.BlockSpec(memory_space=pltpu.HBM)] * hbm,
        out_specs=jax.tree.map(lambda _: pl.BlockSpec(memory_space=pltpu.VMEM), out_shapes),
        scratch_shapes=scratch,
        cost_estimate=cost,
        compiler_params=pltpu.CompilerParams(vmem_limit_bytes=40 * 2**20),
    )


def shape(*dims, dtype=BF):
    return jax.ShapeDtypeStruct(dims, dtype)


def on_device(queries, key_states, value_states, offsets, out_weight):
    n_dev = 128
    planes = [[x * 32 + 2 * j + c for j in range(HEADS)] for x in range(4) for c in range(2)]
    swap = [(i, i ^ 1) for i in range(n_dev)]
    packed = call(
        pack_kernel,
        shape(HEADS, 3 * HDIM, ROWS),
        0,
        3,
        (pltpu.VMEM((3, ROWS, HEADS * HDIM), BF), pltpu.SemaphoreType.DMA((3,))),
    )(*[pltpu.with_memory_space_constraint(a, pltpu.HBM) for a in (queries, key_states, value_states)])
    mine = lax.all_to_all(packed, "seq", 0, 0, axis_index_groups=planes, tiled=True)
    chosen, own_q, own_kv = call(
        select_kernel,
        (shape(5 * HDIM, 128), shape(HDIM, C2 + 128), shape(HEADS, 2 * HDIM, ROWS)),
        2,
    )(offsets, mine)
    other_kv = lax.ppermute(own_kv, "seq", swap)
    units = [chosen]
    for back in (1, 2, 3):
        pairs = [(i, (i + 32 * back) % n_dev) for i in range(n_dev)]
        units.append(lax.ppermute(chosen, "seq", pairs))
    other_q = lax.ppermute(own_q, "seq", swap)
    state = call(
        near_kernel,
        shape(AUG, SEG1, dtype=F32),
        2,
        cost=pl.CostEstimate(flops=6 * 10**9, bytes_accessed=10**7, transcendentals=10**6),
    )(mine, other_kv)
    part = shape(AUG, C2 + 128, dtype=F32)
    sent = call(functools.partial(far_kernel, False), part, 6)(other_q, *units, state)
    kept = call(
        functools.partial(far_kernel, True),
        part,
        6,
        cost=pl.CostEstimate(flops=10**9, bytes_accessed=10**7, transcendentals=10**6),
    )(own_q, *units, state)
    mixed = call(mix_kernel, shape(HEADS, HDIM, ROWS), 4)(
        offsets, state, kept, lax.ppermute(sent, "seq", swap)
    )
    home = lax.all_to_all(mixed, "seq", 0, 0, axis_index_groups=planes, tiled=True)
    return call(project_kernel, shape(ROWS, HEADS * HDIM), 2)(home, out_weight)


def solution(mesh):
    placed = (P("seq", None), P("seq", None), P("seq", None), P(), P())
    return jax.shard_map(
        on_device, mesh=mesh, in_specs=placed, out_specs=P("seq", None), check_vma=False
    )
```

```python
import functools
import math

import jax
import jax.numpy as jnp
from jax import lax
from jax.experimental import pallas as pl
from jax.experimental.pallas import tpu as pltpu
from jax.sharding import PartitionSpec as P

HEADS = 16
HDIM = 80
SEG1 = 2048
SEGS = 8
ROWS = 128
D2 = 8
D3 = 32
C2 = SEG1 // D2
C3 = SEG1 // D3
ROW_L = HDIM
ROW_M = HDIM + 8
AUG = HDIM + 16
SCALE = math.log2(math.e) / math.sqrt(HDIM)
LOW = -1e30
FLOOR = -1e9
IN_ROOT, OUT_ROOT = 14, 10
BF = jnp.bfloat16
F32 = jnp.float32


def listed(root):
    return [(root + n) % HEADS for n in range(HEADS)]


def spot(chip, root):
    return (chip - root) % HEADS


def contract0(a, b):
    return lax.dot_general(a, b, (((0,), (0,)), ((), ())), preferred_element_type=F32)


def dot(a, b):
    return jnp.dot(a, b, preferred_element_type=F32)


def iota(shape, dim):
    return lax.broadcasted_iota(jnp.int32, shape, dim)


def onehot(cond):
    return jnp.where(cond, 1.0, 0.0).astype(BF)


def my_offsets(off_ref):
    head = lax.rem(lax.axis_index("seq") // 2, HEADS)
    mine = jnp.where(iota((2, HEADS), 1) == head, off_ref[...], 0)
    both = jnp.sum(mine, axis=1, keepdims=True)
    return both[:1], both[1:]


def picks(off_ref):
    off2, off3 = my_offsets(off_ref)
    tok = iota((1024, 128), 0)
    lane = iota((1024, 128), 1)
    return jnp.concatenate(
        [onehot(tok == lane * D2 + off2), onehot(tok == lane * D3 + off3)], axis=1
    )


def fold(x):
    return jnp.max(x.reshape(x.shape[0] // 8, 8, x.shape[1]), axis=0)


def blocks(ref, first, low, high):
    return jnp.concatenate(
        [ref[spot(s, IN_ROOT), low:high, :] for s in range(first, first + 8)], axis=1
    )


def pack_kernel(q_hbm, k_hbm, v_hbm, out_ref, held, sems):
    copies = [
        pltpu.make_async_copy(ref, held.at[part], sems.at[part])
        for part, ref in enumerate((q_hbm, k_hbm, v_hbm))
    ]
    for copy in copies:
        copy.start()
    half = HEADS * HDIM // 2
    for part in range(3):
        copies[part].wait()
        for n in range(2):
            turned = held[part, :, n * half : (n + 1) * half].T
            for m in range(8):
                slot = spot(8 * n + m, IN_ROOT)
                out_ref[slot, part * HDIM : (part + 1) * HDIM, :] = turned[
                    m * HDIM : (m + 1) * HDIM
                ]


def select_kernel(off_ref, x_ref, kv_ref, q_ref, all_ref):
    both = jnp.concatenate([blocks(x_ref, 8 * h, 0, 3 * HDIM) for h in range(2)], axis=0)
    got = dot(both, picks(off_ref))
    q0, key0, val0, q1, key1, val1 = [got[n * HDIM : (n + 1) * HDIM] for n in range(6)]
    for n, part in enumerate((key0, key1, val0, val1)):
        kv_ref[n * HDIM : (n + 1) * HDIM, :] = part[:, :128].astype(BF)
    far = key0[:, 128:]
    for n, part in enumerate((key1, val0, val1)):
        far = far + pltpu.roll(part[:, 128:], 32 * (n + 1), 1)
    kv_ref[4 * HDIM :, :] = far.astype(BF)
    q_ref[:, :128] = q0[:, :128].astype(BF)
    q_ref[:, 128:256] = q1[:, :128].astype(BF)
    q_ref[:, 256:] = (q0[:, 128:] + pltpu.roll(q1[:, 128:], 32, 1)).astype(BF)
    for j in range(HEADS):
        all_ref[j] = x_ref[spot(j, IN_ROOT), HDIM:, :]


def near_kernel(x_ref, other_ref, state_ref):
    core = lax.rem(lax.axis_index("seq"), 2)

    def own(s, low, high):
        return x_ref[spot(s, IN_ROOT), low:high, :]

    ones = jnp.ones((16, 256), BF)
    row = iota((256, 256), 0)
    col = iota((256, 256), 1)
    first = col < 128
    last = jnp.where(row < 128, lax.rem(col, 128), 127 + 128 * core)
    diagonal = (row <= jnp.where(first, last, 255), row <= jnp.where(first, -1, last))
    keys = [
        jnp.concatenate([own(s, HDIM, 2 * HDIM), other_ref[s, :HDIM, :]], axis=1).T
        for s in range(HEADS)
    ]

    def score(slot):
        q_t = jnp.concatenate([own(slot + n, 0, HDIM) for n in range(2)], axis=1)
        parts = [dot(keys[n], q_t) for n in range(slot // 8 * 8, slot + 2)]
        for n in range(2):
            parts[n - 2] = jnp.where(diagonal[n], parts[n - 2], LOW)
        return parts

    def weigh(parts):
        top = functools.reduce(jnp.maximum, [fold(p) for p in parts])
        high = jnp.max(top, axis=0, keepdims=True) * SCALE
        return high, [jnp.exp2(p * SCALE - high).astype(BF) for p in parts]

    def gather(slot, high, weights):
        acc = jnp.zeros((AUG, 256), F32)
        for n, part in enumerate(weights):
            s = slot // 8 * 8 + n
            v_t = jnp.concatenate([own(s, 2 * HDIM, 3 * HDIM), other_ref[s, HDIM:, :]], axis=1)
            acc = acc + dot(jnp.concatenate([v_t, ones], axis=0), part)
        cols = slice(slot * 128, (slot + 2) * 128)
        state_ref[:ROW_M, cols] = acc[:ROW_M]
        state_ref[ROW_M:, cols] = jnp.broadcast_to(high, (8, 256))

    order = (6, 14, 4, 12, 2, 10, 0, 8)
    scores = score(order[0])
    waiting = None
    for n, slot in enumerate(order):
        current = scores
        if n + 1 < len(order):
            scores = score(order[n + 1])
        weighed = weigh(current)
        if waiting is not None:
            gather(*waiting)
        waiting = (slot, *weighed)
    gather(*waiting)


def far_kernel(own, q_ref, *refs):
    pieces, out_ref = refs[:4], refs[-1]
    device = lax.axis_index("seq")
    core = lax.rem(device, 2)
    plane = device // 32

    def attend(width, keys, values, q, slot_rows, cols):
        row = iota((width, q.shape[1]), 0)
        col = iota((width, q.shape[1]), 1)
        if own:
            seen = row <= col
        else:
            seen = row // slot_rows < col // slot_rows + 1 - core
        parts, tops, hides = [], [], []
        for n, k_t in enumerate(keys):
            scores = contract0(k_t, q)[:width]
            if n == 0:
                scores = jnp.where(seen, scores, LOW)
            hide = jnp.where(plane >= n, 0.0, LOW).astype(F32)
            parts.append(scores)
            hides.append(hide)
            tops.append(fold(scores) + hide)
        high = jnp.max(functools.reduce(jnp.maximum, tops), axis=0, keepdims=True) * SCALE
        high = jnp.maximum(high, FLOOR).astype(BF).astype(F32)
        acc = jnp.zeros((AUG, q.shape[1]), F32)
        for v_t, scores, hide in zip(values, parts, hides):
            weights = jnp.exp2(scores * SCALE - (high - hide)).astype(BF)
            if v_t.shape[1] > width:
                zeros = jnp.zeros((v_t.shape[1] - width, q.shape[1]), BF)
                weights = jnp.concatenate([zeros, weights], axis=0)
            ones = jnp.ones((16, v_t.shape[1]), BF)
            acc = acc + dot(jnp.concatenate([v_t, ones], axis=0), weights)
        out_ref[:ROW_M, cols] = acc[:ROW_M]
        out_ref[ROW_M:, cols] = jnp.broadcast_to(high, (8, q.shape[1]))

    def pair(piece, n):
        return jnp.concatenate(
            [piece[n * HDIM : (n + 1) * HDIM, :], piece[(n + 1) * HDIM : (n + 2) * HDIM, :]], axis=1
        )

    keys = [pair(p, 0) for p in pieces]
    values = [pair(p, 2) for p in pieces]
    last = [p[4 * HDIM :, :] for p in pieces]
    attend(C2, keys, values, q_ref[:, :C2], ROWS // D2, slice(0, C2))
    attend(C3, last, last, q_ref[:, C2:], ROWS // D3, slice(C2, C2 + 128))


def mix_kernel(off_ref, state_ref, own_ref, other_ref, out_ref):
    off2, off3 = my_offsets(off_ref)
    hi_a, hi_b = own_ref[ROW_M:, :], other_ref[ROW_M:, :]
    high = jnp.maximum(hi_a, hi_b)
    e_a, e_b = jnp.exp2(hi_a - high), jnp.exp2(hi_b - high)
    body = own_ref[:ROW_M, :] * e_a[:1] + other_ref[:ROW_M, :] * e_b[:1]
    top = body.astype(BF)
    rest = (body - top.astype(F32)).astype(BF)
    stat = high.astype(BF)
    top = jnp.concatenate([top, stat], axis=0)
    rest = jnp.concatenate([rest, jnp.zeros_like(stat)], axis=0)
    parts3 = jnp.concatenate([top[:, C2:], rest[:, C2:]], axis=1)
    lane = iota((128, 1024), 0)
    tok = iota((128, 1024), 1)
    place2 = onehot(tok == lane * D2 + off2)
    place2 = jnp.concatenate([place2, place2], axis=0)
    tok1 = iota((1, 1024), 1)
    for half in range(2):
        near = state_ref[:, half * 1024 : (half + 1) * 1024]
        cols = slice(half * 128, (half + 1) * 128)
        lev2 = dot(jnp.concatenate([top[:, cols], rest[:, cols]], axis=1), place2)
        place3 = onehot(tok + half * 1024 == lane * D3 + off3)
        lev3 = dot(parts3, jnp.concatenate([place3, place3], axis=0))
        hi1 = near[ROW_M : ROW_M + 1]
        hi2 = jnp.where(lax.rem(tok1, D2) == off2, lev2[ROW_M : ROW_M + 1], LOW)
        hi3 = jnp.where(lax.rem(tok1, D3) == off3, lev3[ROW_M : ROW_M + 1], LOW)
        peak = jnp.maximum(jnp.maximum(hi1, hi2), hi3)
        shares = [jnp.exp2(hi - peak) for hi in (hi1, hi2, hi3)]
        levels = (near, lev2, lev3)
        total = sum(e * x[ROW_L : ROW_L + 1] for e, x in zip(shares, levels))
        inv = 1.0 / total
        mixed = sum(x[:HDIM] * (e * inv) for e, x in zip(shares, levels)).astype(BF)
        for s in range(8):
            out_ref[spot(half * 8 + s, OUT_ROOT)] = mixed[:, s * 128 : (s + 1) * 128]


def project_kernel(x_ref, w_ref, out_ref):
    x = jnp.concatenate([x_ref[spot(h, OUT_ROOT)] for h in range(HEADS)], axis=0)
    out_ref[...] = contract0(x, w_ref[...]).astype(BF)


def call(kernel, out_shapes, vmem, hbm=0, scratch=(), cost=None):
    return pl.pallas_call(
        kernel,
        out_shape=out_shapes,
        in_specs=[pl.BlockSpec(memory_space=pltpu.VMEM)] * vmem
        + [pl.BlockSpec(memory_space=pltpu.HBM)] * hbm,
        out_specs=jax.tree.map(lambda _: pl.BlockSpec(memory_space=pltpu.VMEM), out_shapes),
        scratch_shapes=scratch,
        cost_estimate=cost,
        compiler_params=pltpu.CompilerParams(vmem_limit_bytes=40 * 2**20),
    )


def shape(*dims, dtype=BF):
    return jax.ShapeDtypeStruct(dims, dtype)


def on_device(queries, key_states, value_states, offsets, out_weight):
    n_dev = 128
    planes = [
        [[x * 32 + 2 * j + c for j in listed(root)] for x in range(4) for c in range(2)]
        for root in (IN_ROOT, OUT_ROOT)
    ]
    swap = [(i, i ^ 1) for i in range(n_dev)]
    packed = call(
        pack_kernel,
        shape(HEADS, 3 * HDIM, ROWS),
        0,
        3,
        (pltpu.VMEM((3, ROWS, HEADS * HDIM), BF), pltpu.SemaphoreType.DMA((3,))),
    )(*[pltpu.with_memory_space_constraint(a, pltpu.HBM) for a in (queries, key_states, value_states)])
    mine = lax.all_to_all(packed, "seq", 0, 0, axis_index_groups=planes[0], tiled=True)
    chosen, own_q, own_kv = call(
        select_kernel,
        (shape(5 * HDIM, 128), shape(HDIM, C2 + 128), shape(HEADS, 2 * HDIM, ROWS)),
        2,
    )(offsets, mine)
    other_kv = lax.ppermute(own_kv, "seq", swap)
    units = [chosen]
    for back in (1, 2, 3):
        pairs = [(i, (i + 32 * back) % n_dev) for i in range(n_dev)]
        units.append(lax.ppermute(chosen, "seq", pairs))
    other_q = lax.ppermute(own_q, "seq", swap)
    state = call(
        near_kernel,
        shape(AUG, SEG1, dtype=F32),
        2,
        cost=pl.CostEstimate(flops=6 * 10**9, bytes_accessed=10**7, transcendentals=10**6),
    )(mine, other_kv)
    part = shape(AUG, C2 + 128, dtype=F32)
    sent = call(functools.partial(far_kernel, False), part, 6)(other_q, *units, state)
    kept = call(
        functools.partial(far_kernel, True),
        part,
        6,
        cost=pl.CostEstimate(flops=10**9, bytes_accessed=10**7, transcendentals=10**6),
    )(own_q, *units, state)
    mixed = call(mix_kernel, shape(HEADS, HDIM, ROWS), 4)(
        offsets, state, kept, lax.ppermute(sent, "seq", swap)
    )
    home = lax.all_to_all(mixed, "seq", 0, 0, axis_index_groups=planes[1], tiled=True)
    return call(project_kernel, shape(ROWS, HEADS * HDIM), 2)(home, out_weight)


def solution(mesh):
    placed = (P("seq", None), P("seq", None), P("seq", None), P(), P())
    return jax.shard_map(
        on_device, mesh=mesh, in_specs=placed, out_specs=P("seq", None), check_vma=False
    )
```

```python
import functools
import math

import jax
import jax.numpy as jnp
from jax import lax
from jax.experimental import pallas as pl
from jax.experimental.pallas import tpu as pltpu
from jax.sharding import PartitionSpec as P

HEADS = 16
HDIM = 80
SEG1 = 2048
SEGS = 8
ROWS = 128
D2 = 8
D3 = 32
C2 = SEG1 // D2
C3 = SEG1 // D3
ROW_L = HDIM
ROW_M = HDIM + 8
AUG = HDIM + 16
SCALE = math.log2(math.e) / math.sqrt(HDIM)
LOW = -1e30
FLOOR = -1e9
IN_ROOT, OUT_ROOT = 14, 10
BF = jnp.bfloat16
F32 = jnp.float32


def listed(root):
    return [(root + n) % HEADS for n in range(HEADS)]


def spot(chip, root):
    return (chip - root) % HEADS


def contract0(a, b):
    return lax.dot_general(a, b, (((0,), (0,)), ((), ())), preferred_element_type=F32)


def dot(a, b):
    return jnp.dot(a, b, preferred_element_type=F32)


def iota(shape, dim):
    return lax.broadcasted_iota(jnp.int32, shape, dim)


def onehot(cond):
    return jnp.where(cond, 1.0, 0.0).astype(BF)


def my_offsets(off_ref):
    head = lax.rem(lax.axis_index("seq") // 2, HEADS)
    mine = jnp.where(iota((2, HEADS), 1) == head, off_ref[...], 0)
    both = jnp.sum(mine, axis=1, keepdims=True)
    return both[:1], both[1:]


def picks(off_ref):
    off2, off3 = my_offsets(off_ref)
    tok = iota((1024, 128), 0)
    lane = iota((1024, 128), 1)
    return jnp.concatenate(
        [onehot(tok == lane * D2 + off2), onehot(tok == lane * D3 + off3)], axis=1
    )


def fold(x):
    return jnp.max(x.reshape(x.shape[0] // 8, 8, x.shape[1]), axis=0)


def blocks(ref, first, low, high):
    return jnp.concatenate(
        [ref[spot(s, IN_ROOT), low:high, :] for s in range(first, first + 8)], axis=1
    )


def pack_kernel(q_hbm, k_hbm, v_hbm, out_ref, held, sems):
    copies = [
        pltpu.make_async_copy(ref, held.at[part], sems.at[part])
        for part, ref in enumerate((q_hbm, k_hbm, v_hbm))
    ]
    for copy in copies:
        copy.start()
    half = HEADS * HDIM // 2
    for part in range(3):
        copies[part].wait()
        for n in range(2):
            turned = held[part, :, n * half : (n + 1) * half].T
            for m in range(8):
                slot = spot(8 * n + m, IN_ROOT)
                out_ref[slot, part * HDIM : (part + 1) * HDIM, :] = turned[
                    m * HDIM : (m + 1) * HDIM
                ]


def select_kernel(off_ref, x_ref, kv_ref, all_ref):
    both = jnp.concatenate([blocks(x_ref, 8 * h, 0, 3 * HDIM) for h in range(2)], axis=0)
    got = dot(both, picks(off_ref))
    q0, key0, val0, q1, key1, val1 = [got[n * HDIM : (n + 1) * HDIM] for n in range(6)]
    for n, part in enumerate((key0, key1, val0, val1)):
        kv_ref[n * HDIM : (n + 1) * HDIM, :] = part[:, :128].astype(BF)
    far = key0[:, 128:]
    for n, part in enumerate((key1, val0, val1)):
        far = far + pltpu.roll(part[:, 128:], 32 * (n + 1), 1)
    kv_ref[4 * HDIM :, :] = far.astype(BF)
    for j in range(HEADS):
        all_ref[j] = x_ref[spot(j, IN_ROOT), HDIM:, :]
    all_ref[HEADS, :HDIM, :] = q0[:, :128].astype(BF)
    all_ref[HEADS, HDIM:, :] = q1[:, :128].astype(BF)
    all_ref[HEADS + 1, :HDIM, :] = (q0[:, 128:] + pltpu.roll(q1[:, 128:], 32, 1)).astype(BF)
    all_ref[HEADS + 1, HDIM:, :] = jnp.zeros((HDIM, 128), BF)


def near_kernel(off_ref, x_ref, other_ref, state_ref, spread_ref):
    core = lax.rem(lax.axis_index("seq"), 2)

    def own(s, low, high):
        return x_ref[spot(s, IN_ROOT), low:high, :]

    ones = jnp.ones((16, 256), BF)
    row = iota((256, 256), 0)
    col = iota((256, 256), 1)
    first = col < 128
    last = jnp.where(row < 128, lax.rem(col, 128), 127 + 128 * core)
    diagonal = (row <= jnp.where(first, last, 255), row <= jnp.where(first, -1, last))
    keys = [
        jnp.concatenate([own(s, HDIM, 2 * HDIM), other_ref[s, :HDIM, :]], axis=1).T
        for s in range(HEADS)
    ]

    def score(slot):
        q_t = jnp.concatenate([own(slot + n, 0, HDIM) for n in range(2)], axis=1)
        parts = [dot(keys[n], q_t) for n in range(slot // 8 * 8, slot + 2)]
        for n in range(2):
            parts[n - 2] = jnp.where(diagonal[n], parts[n - 2], LOW)
        return parts

    def weigh(parts):
        top = functools.reduce(jnp.maximum, [fold(p) for p in parts])
        high = jnp.max(top, axis=0, keepdims=True) * SCALE
        return high, [jnp.exp2(p * SCALE - high).astype(BF) for p in parts]

    def gather(slot, high, weights):
        acc = jnp.zeros((AUG, 256), F32)
        for n, part in enumerate(weights):
            s = slot // 8 * 8 + n
            v_t = jnp.concatenate([own(s, 2 * HDIM, 3 * HDIM), other_ref[s, HDIM:, :]], axis=1)
            acc = acc + dot(jnp.concatenate([v_t, ones], axis=0), part)
        cols = slice(slot * 128, (slot + 2) * 128)
        state_ref[:ROW_M, cols] = acc[:ROW_M]
        state_ref[ROW_M:, cols] = jnp.broadcast_to(high, (8, 256))

    order = (6, 14, 4, 12, 2, 10, 0, 8)
    scores = score(order[0])
    waiting = None
    for n, slot in enumerate(order):
        current = scores
        if n + 1 < len(order):
            scores = score(order[n + 1])
        weighed = weigh(current)
        if waiting is not None:
            gather(*waiting)
        waiting = (slot, *weighed)
    gather(*waiting)
    off2, off3 = my_offsets(off_ref)
    lane = iota((128, 1024), 0)
    tok = iota((128, 1024), 1)
    spread_ref[0] = onehot(tok == lane * D2 + off2)
    for half in range(2):
        spread_ref[1 + half] = onehot(tok + half * 1024 == lax.rem(lane, C3) * D3 + off3)


def far_kernel(own, all_ref, *refs):
    pieces, out_ref = refs[:4], refs[-1]
    device = lax.axis_index("seq")
    core = lax.rem(device, 2)
    plane = device // 32

    def attend(width, keys, values, q, slot_rows, cols):
        row = iota((width, q.shape[1]), 0)
        col = iota((width, q.shape[1]), 1)
        if own:
            seen = row <= col
        else:
            seen = row // slot_rows < col // slot_rows + 1 - core
        parts, tops, hides = [], [], []
        for n, k_t in enumerate(keys):
            scores = contract0(k_t, q)[:width]
            if n == 0:
                scores = jnp.where(seen, scores, LOW)
            hide = jnp.where(plane >= n, 0.0, LOW).astype(F32)
            parts.append(scores)
            hides.append(hide)
            tops.append(fold(scores) + hide)
        high = jnp.max(functools.reduce(jnp.maximum, tops), axis=0, keepdims=True) * SCALE
        high = jnp.maximum(high, FLOOR).astype(BF).astype(F32)
        acc = jnp.zeros((AUG, q.shape[1]), F32)
        for v_t, scores, hide in zip(values, parts, hides):
            weights = jnp.exp2(scores * SCALE - (high - hide)).astype(BF)
            if v_t.shape[1] > width:
                zeros = jnp.zeros((v_t.shape[1] - width, q.shape[1]), BF)
                weights = jnp.concatenate([zeros, weights], axis=0)
            ones = jnp.ones((16, v_t.shape[1]), BF)
            acc = acc + dot(jnp.concatenate([v_t, ones], axis=0), weights)
        out_ref[:ROW_M, cols] = acc[:ROW_M]
        out_ref[ROW_M:, cols] = jnp.broadcast_to(high, (8, q.shape[1]))

    def pair(piece, n):
        return jnp.concatenate(
            [piece[n * HDIM : (n + 1) * HDIM, :], piece[(n + 1) * HDIM : (n + 2) * HDIM, :]], axis=1
        )

    keys = [pair(p, 0) for p in pieces]
    values = [pair(p, 2) for p in pieces]
    last = [p[4 * HDIM :, :] for p in pieces]
    q2 = jnp.concatenate([all_ref[HEADS, :HDIM, :], all_ref[HEADS, HDIM:, :]], axis=1)
    attend(C2, keys, values, q2, ROWS // D2, slice(0, C2))
    q3 = all_ref[HEADS + 1, :HDIM, :]
    attend(C3, last, last, q3, ROWS // D3, slice(C2, C2 + 128))


def mix_kernel(off_ref, state_ref, spread_ref, own_ref, other_ref, out_ref):
    off2, off3 = my_offsets(off_ref)
    hi_a, hi_b = own_ref[ROW_M:, :], other_ref[ROW_M:, :]
    high = jnp.maximum(hi_a, hi_b)
    e_a, e_b = jnp.exp2(hi_a - high), jnp.exp2(hi_b - high)
    body = own_ref[:ROW_M, :] * e_a[:1] + other_ref[:ROW_M, :] * e_b[:1]
    top = body.astype(BF)
    rest = (body - top.astype(F32)).astype(BF)
    stat = high.astype(BF)
    top = jnp.concatenate([top, stat], axis=0)
    rest = jnp.concatenate([rest, jnp.zeros_like(stat)], axis=0)
    parts3 = jnp.concatenate([top[:, C2 : C2 + C3], rest[:, C2 : C2 + C3]], axis=1)
    place2 = jnp.concatenate([spread_ref[0], spread_ref[0]], axis=0)
    tok1 = iota((1, 1024), 1)
    for half in range(2):
        near = state_ref[:, half * 1024 : (half + 1) * 1024]
        cols = slice(half * 128, (half + 1) * 128)
        lev2 = dot(jnp.concatenate([top[:, cols], rest[:, cols]], axis=1), place2)
        lev3 = dot(parts3, spread_ref[1 + half])
        hi1 = near[ROW_M : ROW_M + 1]
        hi2 = jnp.where(lax.rem(tok1, D2) == off2, lev2[ROW_M : ROW_M + 1], LOW)
        hi3 = jnp.where(lax.rem(tok1, D3) == off3, lev3[ROW_M : ROW_M + 1], LOW)
        peak = jnp.maximum(jnp.maximum(hi1, hi2), hi3)
        shares = [jnp.exp2(hi - peak) for hi in (hi1, hi2, hi3)]
        levels = (near, lev2, lev3)
        total = sum(e * x[ROW_L : ROW_L + 1] for e, x in zip(shares, levels))
        inv = 1.0 / total
        mixed = sum(x[:HDIM] * (e * inv) for e, x in zip(shares, levels)).astype(BF)
        for s in range(8):
            out_ref[spot(half * 8 + s, OUT_ROOT)] = mixed[:, s * 128 : (s + 1) * 128]


def project_kernel(x_ref, w_ref, out_hbm, held, sems):
    x = jnp.concatenate([x_ref[spot(h, OUT_ROOT)] for h in range(HEADS)], axis=0)
    copies = []
    for n in range(5):
        cols = slice(n * 256, (n + 1) * 256)
        held[:, cols] = contract0(x, w_ref[:, cols]).astype(BF)
        copy = pltpu.make_async_copy(held.at[:, cols], out_hbm.at[:, cols], sems.at[n])
        copy.start()
        copies.append(copy)
    for copy in copies:
        copy.wait()


def call(kernel, out_shapes, vmem, hbm=0, scratch=(), cost=None, out_space=pltpu.VMEM):
    return pl.pallas_call(
        kernel,
        out_shape=out_shapes,
        in_specs=[pl.BlockSpec(memory_space=pltpu.VMEM)] * vmem
        + [pl.BlockSpec(memory_space=pltpu.HBM)] * hbm,
        out_specs=jax.tree.map(lambda _: pl.BlockSpec(memory_space=out_space), out_shapes),
        scratch_shapes=scratch,
        cost_estimate=cost,
        compiler_params=pltpu.CompilerParams(vmem_limit_bytes=40 * 2**20),
    )


def shape(*dims, dtype=BF):
    return jax.ShapeDtypeStruct(dims, dtype)


def on_device(queries, key_states, value_states, offsets, out_weight):
    n_dev = 128
    planes = [
        [[x * 32 + 2 * j + c for j in listed(root)] for x in range(4) for c in range(2)]
        for root in (IN_ROOT, OUT_ROOT)
    ]
    swap = [(i, i ^ 1) for i in range(n_dev)]
    packed = call(
        pack_kernel,
        shape(HEADS, 3 * HDIM, ROWS),
        0,
        3,
        (pltpu.VMEM((3, ROWS, HEADS * HDIM), BF), pltpu.SemaphoreType.DMA((3,))),
    )(*[pltpu.with_memory_space_constraint(a, pltpu.HBM) for a in (queries, key_states, value_states)])
    mine = lax.all_to_all(packed, "seq", 0, 0, axis_index_groups=planes[0], tiled=True)
    chosen, own_all = call(
        select_kernel, (shape(5 * HDIM, 128), shape(HEADS + 2, 2 * HDIM, ROWS)), 2
    )(offsets, mine)
    other_all = lax.ppermute(own_all, "seq", swap)
    units = [chosen]
    for back in (1, 2, 3):
        pairs = [(i, (i + 32 * back) % n_dev) for i in range(n_dev)]
        units.append(lax.ppermute(chosen, "seq", pairs))
    state, places = call(
        near_kernel,
        (shape(AUG, SEG1, dtype=F32), shape(3, 128, SEG1 // 2)),
        3,
        cost=pl.CostEstimate(flops=6 * 10**9, bytes_accessed=10**7, transcendentals=10**6),
    )(offsets, mine, other_all)
    part = shape(AUG, C2 + 128, dtype=F32)
    sent = call(functools.partial(far_kernel, False), part, 6)(other_all, *units, state)
    kept = call(
        functools.partial(far_kernel, True),
        part,
        6,
        cost=pl.CostEstimate(flops=10**9, bytes_accessed=10**7, transcendentals=10**6),
    )(own_all, *units, state)
    mixed = call(mix_kernel, shape(HEADS, HDIM, ROWS), 5)(
        offsets, state, places, kept, lax.ppermute(sent, "seq", swap)
    )
    home = lax.all_to_all(mixed, "seq", 0, 0, axis_index_groups=planes[1], tiled=True)
    return call(
        project_kernel,
        shape(ROWS, HEADS * HDIM),
        2,
        scratch=(pltpu.VMEM((ROWS, HEADS * HDIM), BF), pltpu.SemaphoreType.DMA((5,))),
        out_space=pltpu.HBM,
    )(home, out_weight)


def solution(mesh):
    placed = (P("seq", None), P("seq", None), P("seq", None), P(), P())
    return jax.shard_map(
        on_device, mesh=mesh, in_specs=placed, out_specs=P("seq", None), check_vma=False
    )
```

```python
import functools
import math

import jax
import jax.numpy as jnp
from jax import lax
from jax.experimental import pallas as pl
from jax.experimental.pallas import tpu as pltpu
from jax.sharding import PartitionSpec as P

HEADS = 16
HDIM = 80
SEG1 = 2048
SEGS = 8
ROWS = 128
D2 = 8
D3 = 32
C2 = SEG1 // D2
C3 = SEG1 // D3
ROW_L = HDIM
ROW_M = HDIM + 8
AUG = HDIM + 16
SCALE = math.log2(math.e) / math.sqrt(HDIM)
LOW = -1e30
FLOOR = -1e9
IN_ROOT = (14, 14)
OUT_ROOT = (13, 10)
BF = jnp.bfloat16
F32 = jnp.float32


def listed(root):
    return [(root + n) % HEADS for n in range(HEADS)]


def spot(chip, roots):
    if roots[0] == roots[1]:
        return (chip - roots[0]) % HEADS
    core = lax.rem(lax.axis_index("seq"), 2)
    return lax.rem(chip + HEADS - roots[0] - (roots[1] - roots[0]) * core, HEADS)


def contract0(a, b):
    return lax.dot_general(a, b, (((0,), (0,)), ((), ())), preferred_element_type=F32)


def dot(a, b):
    return jnp.dot(a, b, preferred_element_type=F32)


def iota(shape, dim):
    return lax.broadcasted_iota(jnp.int32, shape, dim)


def onehot(cond):
    return jnp.where(cond, 1.0, 0.0).astype(BF)


def my_offsets(off_ref):
    head = lax.rem(lax.axis_index("seq") // 2, HEADS)
    mine = jnp.where(iota((2, HEADS), 1) == head, off_ref[...], 0)
    both = jnp.sum(mine, axis=1, keepdims=True)
    return both[:1], both[1:]


def picks(off_ref):
    off2, off3 = my_offsets(off_ref)
    tok = iota((1024, 128), 0)
    lane = iota((1024, 128), 1)
    return jnp.concatenate(
        [onehot(tok == lane * D2 + off2), onehot(tok == lane * D3 + off3)], axis=1
    )


def fold(x):
    return jnp.max(x.reshape(x.shape[0] // 8, 8, x.shape[1]), axis=0)


def blocks(ref, first, low, high):
    return jnp.concatenate(
        [ref[spot(s, IN_ROOT), low:high, :] for s in range(first, first + 8)], axis=1
    )


def pack_kernel(q_hbm, k_hbm, v_hbm, out_ref, held, sems):
    copies = [
        pltpu.make_async_copy(ref, held.at[part], sems.at[part])
        for part, ref in enumerate((q_hbm, k_hbm, v_hbm))
    ]
    for copy in copies:
        copy.start()
    half = HEADS * HDIM // 2
    for part in range(3):
        copies[part].wait()
        for n in range(2):
            turned = held[part, :, n * half : (n + 1) * half].T
            for m in range(8):
                slot = spot(8 * n + m, IN_ROOT)
                out_ref[slot, part * HDIM : (part + 1) * HDIM, :] = turned[
                    m * HDIM : (m + 1) * HDIM
                ]


def select_kernel(off_ref, x_ref, kv_ref, all_ref):
    both = jnp.concatenate([blocks(x_ref, 8 * h, 0, 3 * HDIM) for h in range(2)], axis=0)
    got = dot(both, picks(off_ref))
    q0, key0, val0, q1, key1, val1 = [got[n * HDIM : (n + 1) * HDIM] for n in range(6)]
    for n, part in enumerate((key0, key1, val0, val1)):
        kv_ref[n * HDIM : (n + 1) * HDIM, :] = part[:, :128].astype(BF)
    far = key0[:, 128:]
    for n, part in enumerate((key1, val0, val1)):
        far = far + pltpu.roll(part[:, 128:], 32 * (n + 1), 1)
    kv_ref[4 * HDIM :, :] = far.astype(BF)
    for j in range(HEADS):
        all_ref[j] = x_ref[spot(j, IN_ROOT), HDIM:, :]
    all_ref[HEADS, :HDIM, :] = q0[:, :128].astype(BF)
    all_ref[HEADS, HDIM:, :] = q1[:, :128].astype(BF)
    all_ref[HEADS + 1, :HDIM, :] = (q0[:, 128:] + pltpu.roll(q1[:, 128:], 32, 1)).astype(BF)
    all_ref[HEADS + 1, HDIM:, :] = jnp.zeros((HDIM, 128), BF)


def near_kernel(off_ref, x_ref, other_ref, state_ref, spread_ref):
    core = lax.rem(lax.axis_index("seq"), 2)

    def own(s, low, high):
        return x_ref[spot(s, IN_ROOT), low:high, :]

    ones = jnp.ones((16, 256), BF)
    row = iota((256, 256), 0)
    col = iota((256, 256), 1)
    first = col < 128
    last = jnp.where(row < 128, lax.rem(col, 128), 127 + 128 * core)
    diagonal = (row <= jnp.where(first, last, 255), row <= jnp.where(first, -1, last))
    keys = [
        jnp.concatenate([own(s, HDIM, 2 * HDIM), other_ref[s, :HDIM, :]], axis=1).T
        for s in range(HEADS)
    ]

    def score(slot):
        q_t = jnp.concatenate([own(slot + n, 0, HDIM) for n in range(2)], axis=1)
        parts = [dot(keys[n], q_t) for n in range(slot // 8 * 8, slot + 2)]
        for n in range(2):
            parts[n - 2] = jnp.where(diagonal[n], parts[n - 2], LOW)
        return parts

    def weigh(parts):
        top = functools.reduce(jnp.maximum, [fold(p) for p in parts])
        high = jnp.max(top, axis=0, keepdims=True) * SCALE
        return high, [jnp.exp2(p * SCALE - high).astype(BF) for p in parts]

    def gather(slot, high, weights):
        acc = jnp.zeros((AUG, 256), F32)
        for n, part in enumerate(weights):
            s = slot // 8 * 8 + n
            v_t = jnp.concatenate([own(s, 2 * HDIM, 3 * HDIM), other_ref[s, HDIM:, :]], axis=1)
            acc = acc + dot(jnp.concatenate([v_t, ones], axis=0), part)
        cols = slice(slot * 128, (slot + 2) * 128)
        state_ref[:ROW_M, cols] = acc[:ROW_M]
        state_ref[ROW_M:, cols] = jnp.broadcast_to(high, (8, 256))

    order = (6, 14, 4, 12, 2, 10, 0, 8)
    scores = score(order[0])
    waiting = None
    for n, slot in enumerate(order):
        current = scores
        if n + 1 < len(order):
            scores = score(order[n + 1])
        weighed = weigh(current)
        if waiting is not None:
            gather(*waiting)
        waiting = (slot, *weighed)
    gather(*waiting)
    off2, off3 = my_offsets(off_ref)
    lane = iota((128, 1024), 0)
    tok = iota((128, 1024), 1)
    spread_ref[0] = onehot(tok == lane * D2 + off2)
    for half in range(2):
        spread_ref[1 + half] = onehot(tok + half * 1024 == lax.rem(lane, C3) * D3 + off3)


def far_kernel(own, all_ref, *refs):
    pieces, out_ref = refs[:4], refs[-1]
    device = lax.axis_index("seq")
    core = lax.rem(device, 2)
    plane = device // 32

    def attend(width, keys, values, q, slot_rows, cols):
        row = iota((width, q.shape[1]), 0)
        col = iota((width, q.shape[1]), 1)
        if own:
            seen = row <= col
        else:
            seen = row // slot_rows < col // slot_rows + 1 - core
        parts, tops, hides = [], [], []
        for n, k_t in enumerate(keys):
            scores = contract0(k_t, q)[:width]
            if n == 0:
                scores = jnp.where(seen, scores, LOW)
            hide = jnp.where(plane >= n, 0.0, LOW).astype(F32)
            parts.append(scores)
            hides.append(hide)
            tops.append(fold(scores) + hide)
        high = jnp.max(functools.reduce(jnp.maximum, tops), axis=0, keepdims=True) * SCALE
        high = jnp.maximum(high, FLOOR).astype(BF).astype(F32)
        acc = jnp.zeros((AUG, q.shape[1]), F32)
        for v_t, scores, hide in zip(values, parts, hides):
            weights = jnp.exp2(scores * SCALE - (high - hide)).astype(BF)
            if v_t.shape[1] > width:
                zeros = jnp.zeros((v_t.shape[1] - width, q.shape[1]), BF)
                weights = jnp.concatenate([zeros, weights], axis=0)
            ones = jnp.ones((16, v_t.shape[1]), BF)
            acc = acc + dot(jnp.concatenate([v_t, ones], axis=0), weights)
        out_ref[:ROW_M, cols] = acc[:ROW_M]
        out_ref[ROW_M:, cols] = jnp.broadcast_to(high, (8, q.shape[1]))

    def pair(piece, n):
        return jnp.concatenate(
            [piece[n * HDIM : (n + 1) * HDIM, :], piece[(n + 1) * HDIM : (n + 2) * HDIM, :]], axis=1
        )

    keys = [pair(p, 0) for p in pieces]
    values = [pair(p, 2) for p in pieces]
    last = [p[4 * HDIM :, :] for p in pieces]
    q2 = jnp.concatenate([all_ref[HEADS, :HDIM, :], all_ref[HEADS, HDIM:, :]], axis=1)
    attend(C2, keys, values, q2, ROWS // D2, slice(0, C2))
    q3 = all_ref[HEADS + 1, :HDIM, :]
    attend(C3, last, last, q3, ROWS // D3, slice(C2, C2 + 128))


def mix_kernel(off_ref, state_ref, spread_ref, own_ref, other_ref, out_ref):
    off2, off3 = my_offsets(off_ref)
    hi_a, hi_b = own_ref[ROW_M:, :], other_ref[ROW_M:, :]
    high = jnp.maximum(hi_a, hi_b)
    e_a, e_b = jnp.exp2(hi_a - high), jnp.exp2(hi_b - high)
    body = own_ref[:ROW_M, :] * e_a[:1] + other_ref[:ROW_M, :] * e_b[:1]
    top = body.astype(BF)
    rest = (body - top.astype(F32)).astype(BF)
    stat = high.astype(BF)
    top = jnp.concatenate([top, stat], axis=0)
    rest = jnp.concatenate([rest, jnp.zeros_like(stat)], axis=0)
    parts3 = jnp.concatenate([top[:, C2 : C2 + C3], rest[:, C2 : C2 + C3]], axis=1)
    place2 = jnp.concatenate([spread_ref[0], spread_ref[0]], axis=0)
    tok1 = iota((1, 1024), 1)
    for half in range(2):
        near = state_ref[:, half * 1024 : (half + 1) * 1024]
        cols = slice(half * 128, (half + 1) * 128)
        lev2 = dot(jnp.concatenate([top[:, cols], rest[:, cols]], axis=1), place2)
        lev3 = dot(parts3, spread_ref[1 + half])
        hi1 = near[ROW_M : ROW_M + 1]
        hi2 = jnp.where(lax.rem(tok1, D2) == off2, lev2[ROW_M : ROW_M + 1], LOW)
        hi3 = jnp.where(lax.rem(tok1, D3) == off3, lev3[ROW_M : ROW_M + 1], LOW)
        peak = jnp.maximum(jnp.maximum(hi1, hi2), hi3)
        shares = [jnp.exp2(hi - peak) for hi in (hi1, hi2, hi3)]
        levels = (near, lev2, lev3)
        total = sum(e * x[ROW_L : ROW_L + 1] for e, x in zip(shares, levels))
        inv = 1.0 / total
        mixed = sum(x[:HDIM] * (e * inv) for e, x in zip(shares, levels)).astype(BF)
        for s in range(8):
            out_ref[spot(half * 8 + s, OUT_ROOT)] = mixed[:, s * 128 : (s + 1) * 128]


def project_kernel(x_ref, w_ref, out_hbm, held, sems):
    x = jnp.concatenate([x_ref[spot(h, OUT_ROOT)] for h in range(HEADS)], axis=0)
    copies = []
    for n in range(5):
        cols = slice(n * 256, (n + 1) * 256)
        held[:, cols] = contract0(x, w_ref[:, cols]).astype(BF)
        copy = pltpu.make_async_copy(held.at[:, cols], out_hbm.at[:, cols], sems.at[n])
        copy.start()
        copies.append(copy)
    for copy in copies:
        copy.wait()


def call(kernel, out_shapes, vmem, hbm=0, scratch=(), cost=None, out_space=pltpu.VMEM):
    return pl.pallas_call(
        kernel,
        out_shape=out_shapes,
        in_specs=[pl.BlockSpec(memory_space=pltpu.VMEM)] * vmem
        + [pl.BlockSpec(memory_space=pltpu.HBM)] * hbm,
        out_specs=jax.tree.map(lambda _: pl.BlockSpec(memory_space=out_space), out_shapes),
        scratch_shapes=scratch,
        cost_estimate=cost,
        compiler_params=pltpu.CompilerParams(vmem_limit_bytes=40 * 2**20),
    )


def shape(*dims, dtype=BF):
    return jax.ShapeDtypeStruct(dims, dtype)


def on_device(queries, key_states, value_states, offsets, out_weight):
    n_dev = 128
    planes = [
        [[x * 32 + 2 * j + c for j in listed(roots[c])] for x in range(4) for c in range(2)]
        for roots in (IN_ROOT, OUT_ROOT)
    ]
    swap = [(i, i ^ 1) for i in range(n_dev)]
    packed = call(
        pack_kernel,
        shape(HEADS, 3 * HDIM, ROWS),
        0,
        3,
        (pltpu.VMEM((3, ROWS, HEADS * HDIM), BF), pltpu.SemaphoreType.DMA((3,))),
    )(*[pltpu.with_memory_space_constraint(a, pltpu.HBM) for a in (queries, key_states, value_states)])
    mine = lax.all_to_all(packed, "seq", 0, 0, axis_index_groups=planes[0], tiled=True)
    chosen, own_all = call(
        select_kernel, (shape(5 * HDIM, 128), shape(HEADS + 2, 2 * HDIM, ROWS)), 2
    )(offsets, mine)
    other_all = lax.ppermute(own_all, "seq", swap)
    units = [chosen]
    for back in (1, 2, 3):
        pairs = [(i, (i + 32 * back) % n_dev) for i in range(n_dev)]
        units.append(lax.ppermute(chosen, "seq", pairs))
    state, places = call(
        near_kernel,
        (shape(AUG, SEG1, dtype=F32), shape(3, 128, SEG1 // 2)),
        3,
        cost=pl.CostEstimate(flops=6 * 10**9, bytes_accessed=10**7, transcendentals=10**6),
    )(offsets, mine, other_all)
    part = shape(AUG, C2 + 128, dtype=F32)
    sent = call(functools.partial(far_kernel, False), part, 6)(other_all, *units, state)
    kept = call(
        functools.partial(far_kernel, True),
        part,
        6,
        cost=pl.CostEstimate(flops=10**9, bytes_accessed=10**7, transcendentals=10**6),
    )(own_all, *units, state)
    mixed = call(mix_kernel, shape(HEADS, HDIM, ROWS), 5)(
        offsets, state, places, kept, lax.ppermute(sent, "seq", swap)
    )
    home = lax.all_to_all(mixed, "seq", 0, 0, axis_index_groups=planes[1], tiled=True)
    return call(
        project_kernel,
        shape(ROWS, HEADS * HDIM),
        2,
        scratch=(pltpu.VMEM((ROWS, HEADS * HDIM), BF), pltpu.SemaphoreType.DMA((5,))),
        out_space=pltpu.HBM,
    )(home, out_weight)


def solution(mesh):
    placed = (P("seq", None), P("seq", None), P("seq", None), P(), P())
    return jax.shard_map(
        on_device, mesh=mesh, in_specs=placed, out_specs=P("seq", None), check_vma=False
    )
```

```python
import functools
import math

import jax
import jax.numpy as jnp
from jax import lax
from jax.experimental import pallas as pl
from jax.experimental.pallas import tpu as pltpu
from jax.sharding import PartitionSpec as P

HEADS = 16
HDIM = 80
SEG1 = 2048
SEGS = 8
ROWS = 128
D2 = 8
D3 = 32
C2 = SEG1 // D2
C3 = SEG1 // D3
ROW_L = HDIM
ROW_M = HDIM + 8
AUG = HDIM + 16
SCALE = math.log2(math.e) / math.sqrt(HDIM)
LOW = -1e30
FLOOR = -1e9
IN_ROOT = (13, 14)
OUT_ROOT = (13, 10)
BF = jnp.bfloat16
F32 = jnp.float32


def listed(root):
    return [(root + n) % HEADS for n in range(HEADS)]


def spot(chip, roots):
    if roots[0] == roots[1]:
        return (chip - roots[0]) % HEADS
    core = lax.rem(lax.axis_index("seq"), 2)
    return lax.rem(chip + HEADS - roots[0] - (roots[1] - roots[0]) * core, HEADS)


def contract0(a, b):
    return lax.dot_general(a, b, (((0,), (0,)), ((), ())), preferred_element_type=F32)


def dot(a, b):
    return jnp.dot(a, b, preferred_element_type=F32)


def iota(shape, dim):
    return lax.broadcasted_iota(jnp.int32, shape, dim)


def onehot(cond):
    return jnp.where(cond, 1.0, 0.0).astype(BF)


def my_offsets(off_ref):
    head = lax.rem(lax.axis_index("seq") // 2, HEADS)
    mine = jnp.where(iota((2, HEADS), 1) == head, off_ref[...], 0)
    both = jnp.sum(mine, axis=1, keepdims=True)
    return both[:1], both[1:]


def picks(off_ref):
    off2, off3 = my_offsets(off_ref)
    tok = iota((1024, 128), 0)
    lane = iota((1024, 128), 1)
    return jnp.concatenate(
        [onehot(tok == lane * D2 + off2), onehot(tok == lane * D3 + off3)], axis=1
    )


def fold(x):
    return jnp.max(x.reshape(x.shape[0] // 8, 8, x.shape[1]), axis=0)


def blocks(ref, first, low, high):
    return jnp.concatenate(
        [ref[spot(s, IN_ROOT), low:high, :] for s in range(first, first + 8)], axis=1
    )


def pack_kernel(q_hbm, k_hbm, v_hbm, out_ref, held, sems):
    copies = [
        pltpu.make_async_copy(ref, held.at[part], sems.at[part])
        for part, ref in enumerate((q_hbm, k_hbm, v_hbm))
    ]
    for copy in copies:
        copy.start()
    half = HEADS * HDIM // 2
    for part in range(3):
        copies[part].wait()
        for n in range(2):
            turned = held[part, :, n * half : (n + 1) * half].T
            for m in range(8):
                slot = spot(8 * n + m, IN_ROOT)
                out_ref[slot, part * HDIM : (part + 1) * HDIM, :] = turned[
                    m * HDIM : (m + 1) * HDIM
                ]


def select_kernel(off_ref, x_ref, kv_ref, all_ref):
    both = jnp.concatenate([blocks(x_ref, 8 * h, 0, 3 * HDIM) for h in range(2)], axis=0)
    got = dot(both, picks(off_ref))
    q0, key0, val0, q1, key1, val1 = [got[n * HDIM : (n + 1) * HDIM] for n in range(6)]
    for n, part in enumerate((key0, key1, val0, val1)):
        kv_ref[n * HDIM : (n + 1) * HDIM, :] = part[:, :128].astype(BF)
    far = key0[:, 128:]
    for n, part in enumerate((key1, val0, val1)):
        far = far + pltpu.roll(part[:, 128:], 32 * (n + 1), 1)
    kv_ref[4 * HDIM :, :] = far.astype(BF)
    for j in range(HEADS):
        all_ref[j] = x_ref[spot(j, IN_ROOT), HDIM:, :]
    all_ref[HEADS, :HDIM, :] = q0[:, :128].astype(BF)
    all_ref[HEADS, HDIM:, :] = q1[:, :128].astype(BF)
    all_ref[HEADS + 1, :HDIM, :] = (q0[:, 128:] + pltpu.roll(q1[:, 128:], 32, 1)).astype(BF)
    all_ref[HEADS + 1, HDIM:, :] = jnp.zeros((HDIM, 128), BF)


def near_kernel(off_ref, x_ref, other_ref, state_ref, spread_ref):
    core = lax.rem(lax.axis_index("seq"), 2)

    def own(s, low, high):
        return x_ref[spot(s, IN_ROOT), low:high, :]

    ones = jnp.ones((16, 256), BF)
    row = iota((256, 256), 0)
    col = iota((256, 256), 1)
    first = col < 128
    last = jnp.where(row < 128, lax.rem(col, 128), 127 + 128 * core)
    diagonal = (row <= jnp.where(first, last, 255), row <= jnp.where(first, -1, last))
    keys = [
        jnp.concatenate([own(s, HDIM, 2 * HDIM), other_ref[s, :HDIM, :]], axis=1).T
        for s in range(HEADS)
    ]

    def score(slot):
        q_t = jnp.concatenate([own(slot + n, 0, HDIM) for n in range(2)], axis=1)
        parts = [dot(keys[n], q_t) for n in range(slot // 8 * 8, slot + 2)]
        for n in range(2):
            parts[n - 2] = jnp.where(diagonal[n], parts[n - 2], LOW)
        return parts

    def weigh(parts):
        top = functools.reduce(jnp.maximum, [fold(p) for p in parts])
        high = jnp.max(top, axis=0, keepdims=True) * SCALE
        return high, [jnp.exp2(p * SCALE - high).astype(BF) for p in parts]

    def gather(slot, high, weights):
        acc = jnp.zeros((AUG, 256), F32)
        for n, part in enumerate(weights):
            s = slot // 8 * 8 + n
            v_t = jnp.concatenate([own(s, 2 * HDIM, 3 * HDIM), other_ref[s, HDIM:, :]], axis=1)
            acc = acc + dot(jnp.concatenate([v_t, ones], axis=0), part)
        cols = slice(slot * 128, (slot + 2) * 128)
        state_ref[:ROW_M, cols] = acc[:ROW_M]
        state_ref[ROW_M:, cols] = jnp.broadcast_to(high, (8, 256))

    order = (6, 14, 4, 12, 2, 10, 0, 8)
    scores = score(order[0])
    waiting = None
    for n, slot in enumerate(order):
        current = scores
        if n + 1 < len(order):
            scores = score(order[n + 1])
        weighed = weigh(current)
        if waiting is not None:
            gather(*waiting)
        waiting = (slot, *weighed)
    gather(*waiting)
    off2, off3 = my_offsets(off_ref)
    lane = iota((128, 1024), 0)
    tok = iota((128, 1024), 1)
    spread_ref[0] = onehot(tok == lane * D2 + off2)
    for half in range(2):
        spread_ref[1 + half] = onehot(tok + half * 1024 == lax.rem(lane, C3) * D3 + off3)


def far_kernel(own, all_ref, *refs):
    pieces, out_ref = refs[:4], refs[-1]
    device = lax.axis_index("seq")
    core = lax.rem(device, 2)
    plane = device // 32

    def attend(width, keys, values, q, slot_rows, cols):
        row = iota((width, q.shape[1]), 0)
        col = iota((width, q.shape[1]), 1)
        if own:
            seen = row <= col
        else:
            seen = row // slot_rows < col // slot_rows + 1 - core
        parts, tops, hides = [], [], []
        for n, k_t in enumerate(keys):
            scores = contract0(k_t, q)[:width]
            if n == 0:
                scores = jnp.where(seen, scores, LOW)
            hide = jnp.where(plane >= n, 0.0, LOW).astype(F32)
            parts.append(scores)
            hides.append(hide)
            tops.append(fold(scores) + hide)
        high = jnp.max(functools.reduce(jnp.maximum, tops), axis=0, keepdims=True) * SCALE
        high = jnp.maximum(high, FLOOR).astype(BF).astype(F32)
        acc = jnp.zeros((AUG, q.shape[1]), F32)
        for v_t, scores, hide in zip(values, parts, hides):
            weights = jnp.exp2(scores * SCALE - (high - hide)).astype(BF)
            if v_t.shape[1] > width:
                zeros = jnp.zeros((v_t.shape[1] - width, q.shape[1]), BF)
                weights = jnp.concatenate([zeros, weights], axis=0)
            ones = jnp.ones((16, v_t.shape[1]), BF)
            acc = acc + dot(jnp.concatenate([v_t, ones], axis=0), weights)
        out_ref[:ROW_M, cols] = acc[:ROW_M]
        out_ref[ROW_M:, cols] = jnp.broadcast_to(high, (8, q.shape[1]))

    def pair(piece, n):
        return jnp.concatenate(
            [piece[n * HDIM : (n + 1) * HDIM, :], piece[(n + 1) * HDIM : (n + 2) * HDIM, :]], axis=1
        )

    keys = [pair(p, 0) for p in pieces]
    values = [pair(p, 2) for p in pieces]
    last = [p[4 * HDIM :, :] for p in pieces]
    q2 = jnp.concatenate([all_ref[HEADS, :HDIM, :], all_ref[HEADS, HDIM:, :]], axis=1)
    attend(C2, keys, values, q2, ROWS // D2, slice(0, C2))
    q3 = all_ref[HEADS + 1, :HDIM, :]
    attend(C3, last, last, q3, ROWS // D3, slice(C2, C2 + 128))


def mix_kernel(off_ref, state_ref, spread_ref, own_ref, other_ref, out_ref):
    off2, off3 = my_offsets(off_ref)
    hi_a, hi_b = own_ref[ROW_M:, :], other_ref[ROW_M:, :]
    high = jnp.maximum(hi_a, hi_b)
    e_a, e_b = jnp.exp2(hi_a - high), jnp.exp2(hi_b - high)
    body = own_ref[:ROW_M, :] * e_a[:1] + other_ref[:ROW_M, :] * e_b[:1]
    top = body.astype(BF)
    rest = (body - top.astype(F32)).astype(BF)
    stat = high.astype(BF)
    top = jnp.concatenate([top, stat], axis=0)
    rest = jnp.concatenate([rest, jnp.zeros_like(stat)], axis=0)
    parts3 = jnp.concatenate([top[:, C2 : C2 + C3], rest[:, C2 : C2 + C3]], axis=1)
    place2 = jnp.concatenate([spread_ref[0], spread_ref[0]], axis=0)
    tok1 = iota((1, 1024), 1)
    for half in range(2):
        near = state_ref[:, half * 1024 : (half + 1) * 1024]
        cols = slice(half * 128, (half + 1) * 128)
        lev2 = dot(jnp.concatenate([top[:, cols], rest[:, cols]], axis=1), place2)
        lev3 = dot(parts3, spread_ref[1 + half])
        hi1 = near[ROW_M : ROW_M + 1]
        hi2 = jnp.where(lax.rem(tok1, D2) == off2, lev2[ROW_M : ROW_M + 1], LOW)
        hi3 = jnp.where(lax.rem(tok1, D3) == off3, lev3[ROW_M : ROW_M + 1], LOW)
        peak = jnp.maximum(jnp.maximum(hi1, hi2), hi3)
        shares = [jnp.exp2(hi - peak) for hi in (hi1, hi2, hi3)]
        levels = (near, lev2, lev3)
        total = sum(e * x[ROW_L : ROW_L + 1] for e, x in zip(shares, levels))
        inv = 1.0 / total
        mixed = sum(x[:HDIM] * (e * inv) for e, x in zip(shares, levels)).astype(BF)
        for s in range(8):
            out_ref[spot(half * 8 + s, OUT_ROOT)] = mixed[:, s * 128 : (s + 1) * 128]


def project_kernel(x_ref, w_ref, out_hbm, held, sems):
    x = jnp.concatenate([x_ref[spot(h, OUT_ROOT)] for h in range(HEADS)], axis=0)
    copies = []
    for n in range(5):
        cols = slice(n * 256, (n + 1) * 256)
        held[:, cols] = contract0(x, w_ref[:, cols]).astype(BF)
        copy = pltpu.make_async_copy(held.at[:, cols], out_hbm.at[:, cols], sems.at[n])
        copy.start()
        copies.append(copy)
    for copy in copies:
        copy.wait()


def call(kernel, out_shapes, vmem, hbm=0, scratch=(), cost=None, out_space=pltpu.VMEM):
    return pl.pallas_call(
        kernel,
        out_shape=out_shapes,
        in_specs=[pl.BlockSpec(memory_space=pltpu.VMEM)] * vmem
        + [pl.BlockSpec(memory_space=pltpu.HBM)] * hbm,
        out_specs=jax.tree.map(lambda _: pl.BlockSpec(memory_space=out_space), out_shapes),
        scratch_shapes=scratch,
        cost_estimate=cost,
        compiler_params=pltpu.CompilerParams(vmem_limit_bytes=40 * 2**20),
    )


def shape(*dims, dtype=BF):
    return jax.ShapeDtypeStruct(dims, dtype)


def on_device(queries, key_states, value_states, offsets, out_weight):
    n_dev = 128
    planes = [
        [[x * 32 + 2 * j + c for j in listed(roots[c])] for x in range(4) for c in range(2)]
        for roots in (IN_ROOT, OUT_ROOT)
    ]
    swap = [(i, i ^ 1) for i in range(n_dev)]
    packed = call(
        pack_kernel,
        shape(HEADS, 3 * HDIM, ROWS),
        0,
        3,
        (pltpu.VMEM((3, ROWS, HEADS * HDIM), BF), pltpu.SemaphoreType.DMA((3,))),
    )(*[pltpu.with_memory_space_constraint(a, pltpu.HBM) for a in (queries, key_states, value_states)])
    mine = lax.all_to_all(packed, "seq", 0, 0, axis_index_groups=planes[0], tiled=True)
    chosen, own_all = call(
        select_kernel, (shape(5 * HDIM, 128), shape(HEADS + 2, 2 * HDIM, ROWS)), 2
    )(offsets, mine)
    other_all = lax.ppermute(own_all, "seq", swap)
    units = [chosen]
    for back in (1, 2, 3):
        pairs = [(i, (i + 32 * back) % n_dev) for i in range(n_dev)]
        units.append(lax.ppermute(chosen, "seq", pairs))
    state, places = call(
        near_kernel,
        (shape(AUG, SEG1, dtype=F32), shape(3, 128, SEG1 // 2)),
        3,
        cost=pl.CostEstimate(flops=6 * 10**9, bytes_accessed=10**7, transcendentals=10**6),
    )(offsets, mine, other_all)
    part = shape(AUG, C2 + 128, dtype=F32)
    sent = call(functools.partial(far_kernel, False), part, 6)(other_all, *units, state)
    kept = call(
        functools.partial(far_kernel, True),
        part,
        6,
        cost=pl.CostEstimate(flops=10**9, bytes_accessed=10**7, transcendentals=10**6),
    )(own_all, *units, state)
    mixed = call(mix_kernel, shape(HEADS, HDIM, ROWS), 5)(
        offsets, state, places, kept, lax.ppermute(sent, "seq", swap)
    )
    home = lax.all_to_all(mixed, "seq", 0, 0, axis_index_groups=planes[1], tiled=True)
    return call(
        project_kernel,
        shape(ROWS, HEADS * HDIM),
        2,
        scratch=(pltpu.VMEM((ROWS, HEADS * HDIM), BF), pltpu.SemaphoreType.DMA((5,))),
        out_space=pltpu.HBM,
    )(home, out_weight)


def solution(mesh):
    placed = (P("seq", None), P("seq", None), P("seq", None), P(), P())
    return jax.shard_map(
        on_device, mesh=mesh, in_specs=placed, out_specs=P("seq", None), check_vma=False
    )
```
